32 devices in a mesh: dp: 4 (over y, x), tensor: 8 (over z, core).
Axes of the slice: x: 2, y: 2, z: 4, core: 2. Of those that a mesh axis runs over, the one named last changes fastest.
Arguments:
- tokens: bfloat16 [1536, 8192], P('dp', 'tensor'), may hold values from -6 to 6
- cotangent: bfloat16 [1536, 8192], P('dp', 'tensor'), may hold values from -6 to 6
- gate_weight: bfloat16 [8192, 14336], P(None, 'tensor'), may hold values from -0.09375 to 0.09375
- up_weight: bfloat16 [8192, 14336], P(None, 'tensor'), may hold values from -0.09375 to 0.09375
- down_weight: bfloat16 [14336, 8192], P('tensor'), may hold values from -0.0625 to 0.0625
- block_task: int32 [12], P('dp'), may hold values from 0 to 63
- block_fill: int32 [12], P('dp'), may hold values from 1 to 128
- task_slot: int32 [64], replicated, may hold values from 0 to 63, each once
- inner_correction_weights: bfloat16 [64, 64, 8192], P('dp', None, 'tensor'), may hold values from -0.0625 to 0.0625
- up_b: bfloat16 [64, 64, 14336], P('dp', None, 'tensor'), may hold values from -0.75 to 0.75
Outputs:
- mixed: bfloat16 [1536, 8192], P('dp', 'tensor')
- item_derivative: bfloat16 [1536, 8192], P('dp', 'tensor')
- up_a_grad: bfloat16 [64, 64, 8192], P('dp', None, 'tensor')
- up_b_grad: bfloat16 [64, 64, 14336], P('dp', None, 'tensor')
The draws below stay inside these ranges and needn't reach their ends.
Inputs may be any that keep to these rules, and one draw needn't show every extreme that they name: `task_slot`: slot s is held by data group s // 16.
All inputs are finite; a program needn't handle non-finite values.
Results may differ from the reference program's by a relative error of at most 0.019.
Values may be sent and summed in bfloat16 or wider, within the bound.
No kernel may reach another device: no remote copies, remote signals or barrier semaphores. Data moves between devices by JAX's collectives and lax.ppermute only.
A program may use at most 192 MiB of HBM per device.

```python
import math
import jax
import jax.numpy as jnp
import numpy as np
from jax import lax

FEATURE_COUNT = 8192
HIDDEN_UNITS = 14336
R = 64
TASKS = 64
BLOCK = 128
ITEM_COUNT = 1536
BLOCKS = 12
N_TENSOR = 8


def plant(values, own_key, least, top_value):
    longest = values.shape.index(max(values.shape))
    spots = []
    for shift in (0, 1):
        where = [jax.random.randint(jax.random.fold_in(own_key, axis), (), 0, length) for axis, length in enumerate(values.shape)]
        where[longest] = (where[longest] + shift) % values.shape[longest]
        spots.append(tuple(where))
    return values.at[spots[0]].set(least).at[spots[1]].set(top_value)


def spiked(array, stream_key, source, target, blocks, factor):
    def block_of(dim):
        return (jnp.arange(array.shape[dim]) // (array.shape[dim] // blocks)).reshape((-1,) + (1,) * (array.ndim - 1 - dim))

    one_side = jax.random.permutation(stream_key, blocks)[block_of(target)]
    second = (block_of(target) + blocks // 2) % blocks
    return jnp.where((block_of(source) == one_side) | (block_of(source) == second), factor * array, array)


def steps_of(rng, shape, pieces, smallest, high):
    def one(position, blocks):
        draws = jax.random.uniform(jax.random.fold_in(jax.random.fold_in(rng, 6), position), (blocks,), jnp.float32, smallest / len(pieces), high / len(pieces))
        return jnp.repeat(jnp.exp(draws), shape[position] // blocks).reshape((-1,) + (1,) * (len(shape) - position - 1))

    factor_of = one(*pieces[0])
    for cut in pieces[1:]:
        factor_of = factor_of * one(*cut)
    return factor_of


def rank_table(number_of, skew):
    loads = [(1 << 20) // math.isqrt(grade ** skew) + 1 for grade in range(1, number_of + 1)]
    scale = 1 + sum(loads) // (1 << 30)
    return np.cumsum(np.array([max(1, weight // scale) for weight in loads]))


def ranked_ids(own_key, extent, count, slope):
    listing = rank_table(count, slope)
    ticket = jax.random.randint(jax.random.fold_in(own_key, 1), extent, 0, int(listing[count - 1]))
    grade = jnp.searchsorted(jnp.asarray(listing, jnp.int32), ticket, side="right")
    return jax.random.permutation(jax.random.fold_in(own_key, 2), count)[grade].astype(jnp.int32)


def bell_draw(stream_key, shape, deviation, reach, split=(), kind=jnp.bfloat16):
    loudness = steps_of(stream_key, shape, split, -0.22, 0.18) if split else 1.0
    entries = jax.random.normal(stream_key, shape, jnp.float32) * deviation * loudness
    return jnp.minimum(jnp.maximum(entries, -reach), reach).astype(kind)


def heavy_noise(rng, dims, deviation, most, cuts, heavy, held_as=jnp.bfloat16):
    values = deviation * jax.random.normal(rng, dims, jnp.float32)
    if cuts:
        values = values * steps_of(rng, dims, cuts, -0.22, 0.18)
    return jnp.clip(spiked(values, jax.random.fold_in(rng, 3), *heavy), -most, most).astype(held_as)


def setup_inputs(seed: int = 0) -> dict:
    key_list = jax.random.split(jax.random.key(seed), 11)
    return {
        "tokens": bell_draw(key_list[0], (ITEM_COUNT, FEATURE_COUNT), 1.0, 6.0, ((0, 4), (1, 8))),
        "cotangent": bell_draw(key_list[1], (ITEM_COUNT, FEATURE_COUNT), 1.0, 6.0, ((0, 4), (1, 8))),
        "gate_weight": heavy_noise(key_list[2], (FEATURE_COUNT, HIDDEN_UNITS), FEATURE_COUNT ** -0.5, 0.09375, ((1, 8),), (1, 0, 8, 2.0)),
        "up_weight": heavy_noise(key_list[3], (FEATURE_COUNT, HIDDEN_UNITS), FEATURE_COUNT ** -0.5, 0.09375, ((1, 8),), (1, 0, 8, 2.0)),
        "down_weight": heavy_noise(key_list[4], (HIDDEN_UNITS, FEATURE_COUNT), HIDDEN_UNITS ** -0.5, 0.0625, ((0, 8),), (0, 1, 8, 2.0)),
        "block_task": plant(ranked_ids(key_list[5], (BLOCKS,), TASKS, 2), jax.random.fold_in(key_list[5], 3), 0, TASKS - 1).astype(jnp.int32),
        "block_fill": plant(jax.random.randint(key_list[6], (BLOCKS,), 1, BLOCK + 1), jax.random.fold_in(key_list[6], 1), 1, BLOCK).astype(jnp.int32),
        "task_slot": jax.random.permutation(key_list[7], TASKS).astype(jnp.int32),
        "inner_correction_weights": bell_draw(key_list[8], (TASKS, R, FEATURE_COUNT), FEATURE_COUNT ** -0.5, 0.0625, ((0, 4), (2, 8))),
        "up_b": bell_draw(key_list[9], (TASKS, R, HIDDEN_UNITS), R ** -0.5, 0.75, ((0, 4), (2, 8))),
    }


adapter_scale = 0.25


def group_sum(pairs, width):
    row_total = pairs[0][0].shape[0]
    col_total = pairs[0][1].shape[1]

    def add_group(group, total):
        begin = (group * width).astype(jnp.int32)
        part = jnp.zeros((row_total, col_total), jnp.float32)
        for left, right in pairs:
            left_piece = lax.dynamic_slice_in_dim(left, begin, width, 1)
            right_piece = lax.dynamic_slice_in_dim(right, begin, width, 0)
            part = part + jnp.dot(left_piece, right_piece, preferred_element_type=jnp.float32)
        rounded = lax.optimization_barrier(part.astype(jnp.bfloat16))
        return total + rounded.astype(jnp.float32)

    return lax.fori_loop(0, N_TENSOR, add_group, jnp.zeros((row_total, col_total), jnp.float32))


def reference(tokens, cotangent, gate_weight, up_weight, down_weight, block_task, block_fill, task_slot, inner_correction_weights, up_b):
    block_count = ITEM_COUNT // BLOCK
    width = HIDDEN_UNITS // N_TENSOR
    segment_owner_index = task_slot[block_task].astype(jnp.int32)
    enabled_flags = (jnp.arange(BLOCK, dtype=jnp.int32)[None, :] < block_fill[:, None]).astype(jnp.float32)[..., None]
    portion_clusters = tokens.reshape(block_count, BLOCK, FEATURE_COUNT).astype(jnp.float32)
    correction_source_vector = inner_correction_weights[segment_owner_index].astype(jnp.float32)
    up_factor_output = up_b[segment_owner_index].astype(jnp.float32)
    gate = jnp.dot(tokens, gate_weight, preferred_element_type=jnp.float32)
    locked_raise_values = jnp.dot(tokens, up_weight, preferred_element_type=jnp.float32)
    narrow_product = jnp.einsum("imk,iok->imo", portion_clusters, correction_source_vector) * enabled_flags
    low_rank_b_output = narrow_product.astype(jnp.bfloat16)
    adapter_up_output = jnp.einsum("vam,vmk->vak", low_rank_b_output.astype(jnp.float32), up_factor_output).reshape(ITEM_COUNT, HIDDEN_UNITS)
    up_projection = locked_raise_values + adapter_scale * adapter_up_output
    sigmoid_gate = jax.nn.sigmoid(gate)
    activated = gate * sigmoid_gate
    hidden = (activated * up_projection).astype(jnp.bfloat16)
    mixed = group_sum([(hidden, down_weight)], width).astype(jnp.bfloat16)
    d_hidden = jnp.dot(cotangent, down_weight.T, preferred_element_type=jnp.float32)
    d_gate = (d_hidden * up_projection * sigmoid_gate * (1.0 + gate * (1.0 - sigmoid_gate))).astype(jnp.bfloat16)
    d_up = (d_hidden * activated).astype(jnp.bfloat16)
    gradient_per_block = d_up.reshape(block_count, BLOCK, HIDDEN_UNITS).astype(jnp.float32)
    narrow_derivative = adapter_scale * jnp.einsum("oge,oce->ogc", gradient_per_block, up_factor_output) * enabled_flags
    exterior_multiplier_dual = narrow_derivative.astype(jnp.bfloat16).astype(jnp.float32)
    fixed_weight_derivative = group_sum([(d_gate, gate_weight.T), (d_up, up_weight.T)], width)
    adjoint_of_correction = jnp.einsum("lxu,luz->lxz", exterior_multiplier_dual, correction_source_vector).reshape(ITEM_COUNT, FEATURE_COUNT)
    item_derivative = (fixed_weight_derivative + adjoint_of_correction).astype(jnp.bfloat16)
    one_hot = (segment_owner_index[:, None] == jnp.arange(TASKS, dtype=jnp.int32)[None, :]).astype(jnp.float32)
    arriving_slope = jnp.einsum("bqf,bqm->bfm", exterior_multiplier_dual, portion_clusters)
    output_gradient = adapter_scale * jnp.einsum("wvd,wvg->wdg", low_rank_b_output.astype(jnp.float32), gradient_per_block)
    up_a_grad = jnp.einsum("bs,brd->srd", one_hot, arriving_slope, precision=lax.Precision.HIGHEST).astype(jnp.bfloat16)
    up_b_grad = jnp.einsum("bs,brf->srf", one_hot, output_gradient, precision=lax.Precision.HIGHEST).astype(jnp.bfloat16)
    return mixed, item_derivative, up_a_grad, up_b_grad
```

```python
import functools

import jax
import jax.numpy as jnp
from jax import lax
from jax.experimental import pallas as pl
from jax.experimental.pallas import tpu as pltpu
from jax.sharding import PartitionSpec as P

BLOCK = 128
adapter_scale = 0.25
VMEM_LIMIT = 32 * 1024 * 1024
COVER = 1 << 32
f32 = jnp.float32
bf16 = jnp.bfloat16
NT = (((1,), (1,)), ((), ()))


def params():
    return pltpu.CompilerParams(vmem_limit_bytes=VMEM_LIMIT)


def tile_of(size, most=256):
    return next((t for t in range(most, 127, -128) if size % t == 0), size)


def ordered_call(kernel, *, grid, in_specs, out_specs, out_shape, name, flops=1 << 27, prefetch=0, scratch=(), after=()):
    many = prefetch + len(in_specs)
    outs = len(out_specs)

    def run(*refs):
        mark = refs[many + len(after) + outs]
        mark[...] = jnp.zeros_like(mark)
        kernel(*refs[:many], *refs[many + len(after) : many + len(after) + outs], *refs[many + len(after) + outs + 1 :])

    call = pl.pallas_call(
        run,
        grid_spec=pltpu.PrefetchScalarGridSpec(
            num_scalar_prefetch=prefetch,
            grid=grid,
            in_specs=list(in_specs) + [pl.BlockSpec(memory_space=pl.ANY)] * len(after),
            out_specs=list(out_specs) + [pl.BlockSpec((8, 128), lambda *_: (0, 0))],
            scratch_shapes=list(scratch),
        ),
        out_shape=list(out_shape) + [jax.ShapeDtypeStruct((8, 128), f32)],
        compiler_params=params(),
        cost_estimate=pl.CostEstimate(flops=flops, bytes_accessed=flops // 384, transcendentals=0),
        name=name,
    )
    return lambda *operands: call(*operands, *after)


def adapter_rows(count):
    return [slice(i * BLOCK, (i + 1) * BLOCK) for i in range(count)]


def forward_part(ids, shards, gate_weight, up_weight, sums, after):
    rows, width = shards[0].shape
    hidden = gate_weight.shape[1]
    tile = tile_of(hidden)
    many = len(shards)

    def kernel(ids_ref, *refs):
        xs, gs, us = refs[:many], refs[many : 2 * many], refs[2 * many : 3 * many]
        g = u = None
        if sums:
            g, u = refs[3 * many][...], refs[3 * many + 1][...]
        for x, wg, wu in zip(xs, gs, us):
            a = x[...]
            pg = jnp.dot(a, wg[...], preferred_element_type=f32)
            pu = jnp.dot(a, wu[...], preferred_element_type=f32)
            g, u = (pg, pu) if g is None else (g + pg, u + pu)
        refs[-2][...] = g
        refs[-1][...] = u

    whole = pl.BlockSpec((rows, width), lambda t, ids: (0, 0))
    weights = [pl.BlockSpec((width, tile), lambda t, ids, i=i: (ids[i], t)) for i in range(many)]
    acc = pl.BlockSpec((rows, tile), lambda t, ids: (0, t))
    shape = jax.ShapeDtypeStruct((rows, hidden), f32)
    return ordered_call(
        kernel,
        prefetch=1,
        grid=(hidden // tile,),
        in_specs=[whole] * many + weights + weights + [acc] * len(sums),
        out_specs=[acc, acc],
        out_shape=[shape, shape],
        name="forward_part",
        flops=4 * many * rows * width * hidden,
        after=after,
    )(ids, *shards, *[gate_weight] * many, *[up_weight] * many, *sums)


def activate(gate, up, low_b, factor, after):
    rows, hidden = gate.shape
    tile = tile_of(hidden, 512)
    count, rank = factor.shape[0], factor.shape[1]

    def kernel(g_ref, u_ref, low_ref, b_ref, h_ref, act_ref, slope_ref):
        for i, part in enumerate(adapter_rows(count)):
            g = g_ref[part]
            u = u_ref[part] + adapter_scale * jnp.dot(low_ref[part], b_ref[i], preferred_element_type=f32)
            s = jax.nn.sigmoid(g)
            act = g * s
            act_ref[part] = act
            h_ref[part] = (act * u).astype(bf16)
            slope_ref[part] = u * s * (1.0 + g * (1.0 - s))

    acc = pl.BlockSpec((rows, tile), lambda t: (0, t))
    return ordered_call(
        kernel,
        grid=(hidden // tile,),
        in_specs=[
            acc, acc,
            pl.BlockSpec((rows, rank), lambda t: (0, 0)),
            pl.BlockSpec((count, rank, tile), lambda t: (0, 0, t)),
        ],
        out_specs=[acc, acc, acc],
        out_shape=[
            jax.ShapeDtypeStruct((rows, hidden), bf16),
            jax.ShapeDtypeStruct((rows, hidden), f32),
            jax.ShapeDtypeStruct((rows, hidden), f32),
        ],
        name="activate",
        flops=1 << 31,
        after=after,
    )(gate, up, low_b, factor)


def hidden_product(x_refs, w_refs):
    return functools.reduce(
        jnp.add,
        [lax.dot_general(x[...], w[...], NT, preferred_element_type=f32) for x, w in zip(x_refs, w_refs)],
    )


def hidden_part(ids, shards, down_weight, after):
    rows, width = shards[0].shape
    hidden = down_weight.shape[0]
    tile = tile_of(hidden)
    many = len(shards)

    def kernel(ids_ref, *refs):
        refs[-1][...] = hidden_product(refs[:many], refs[many:-1])

    whole = pl.BlockSpec((rows, width), lambda t, ids: (0, 0))
    weights = [pl.BlockSpec((tile, width), lambda t, ids, i=i: (t, ids[i])) for i in range(many)]
    return ordered_call(
        kernel,
        prefetch=1,
        grid=(hidden // tile,),
        in_specs=[whole] * many + weights,
        out_specs=[pl.BlockSpec((rows, tile), lambda t, ids: (0, t))],
        out_shape=[jax.ShapeDtypeStruct((rows, hidden), f32)],
        name="hidden_part",
        flops=2 * many * rows * width * hidden,
        after=after,
    )(ids, *shards, *([down_weight] * many))


def hidden_gradients(ids, shards, down_weight, total, act, slope, low_b, factor, after):
    rows, width = shards[0].shape
    hidden = down_weight.shape[0]
    tile = tile_of(hidden)
    count, rank = factor.shape[0], factor.shape[1]
    many = len(shards)

    def kernel(ids_ref, *refs):
        d_ref, act_ref, slope_ref, low_ref, b_ref, dg_ref, du_ref, dl_ref, gb_ref = refs[2 * many :]
        d = d_ref[...] + hidden_product(refs[:many], refs[many : 2 * many])
        dg_ref[...] = (d * slope_ref[...]).astype(bf16)
        du = (d * act_ref[...]).astype(bf16)
        du_ref[...] = du

        @pl.when(pl.program_id(0) == 0)
        def _():
            dl_ref[...] = jnp.zeros_like(dl_ref)

        for i, part in enumerate(adapter_rows(count)):
            dl_ref[part] += lax.dot_general(du[part], b_ref[i], NT, preferred_element_type=f32)
            grad = lax.dot_general(low_ref[part], du[part], (((0,), (0,)), ((), ())), preferred_element_type=f32)
            gb_ref[i] = (adapter_scale * grad).astype(bf16)

    whole = pl.BlockSpec((rows, width), lambda t, ids: (0, 0))
    weights = [pl.BlockSpec((tile, width), lambda t, ids, i=i: (t, ids[i])) for i in range(many)]
    acc = pl.BlockSpec((rows, tile), lambda t, ids: (0, t))
    lows = pl.BlockSpec((rows, rank), lambda t, ids: (0, 0))
    factors = pl.BlockSpec((count, rank, tile), lambda t, ids: (0, 0, t))
    return ordered_call(
        kernel,
        prefetch=1,
        grid=(hidden // tile,),
        in_specs=[whole] * many + weights + [acc, acc, acc, lows, factors],
        out_specs=[acc, acc, lows, factors],
        out_shape=[
            jax.ShapeDtypeStruct((rows, hidden), bf16),
            jax.ShapeDtypeStruct((rows, hidden), bf16),
            jax.ShapeDtypeStruct((rows, rank), f32),
            jax.ShapeDtypeStruct((count, rank, hidden), bf16),
        ],
        name="hidden_gradients",
        flops=2 * many * rows * width * hidden,
        after=after,
    )(ids, *shards, *([down_weight] * many), total, act, slope, low_b, factor)


def mixed_parts(ids, x, down_weight, width, after):
    rows, hidden = x.shape
    tile = tile_of(width, 512)
    steps = width // tile
    pairs = ids.shape[0] // 2

    def kernel(ids_ref, x_ref, wa, wb, oa, ob):
        oa[0] = jnp.dot(x_ref[...], wa[...], preferred_element_type=f32).astype(bf16)
        ob[0] = jnp.dot(x_ref[...], wb[...], preferred_element_type=f32).astype(bf16)

    out = pl.BlockSpec((1, rows, tile), lambda j, t, ids: (j, 0, t))
    shape = jax.ShapeDtypeStruct((pairs, rows, width), bf16)
    return ordered_call(
        kernel,
        prefetch=1,
        grid=(pairs, steps),
        in_specs=[
            pl.BlockSpec((rows, hidden), lambda j, t, ids: (0, 0)),
            pl.BlockSpec((hidden, tile), lambda j, t, ids: (0, ids[2 * j] * steps + t)),
            pl.BlockSpec((hidden, tile), lambda j, t, ids: (0, ids[2 * j + 1] * steps + t)),
        ],
        out_specs=[out, out],
        out_shape=[shape, shape],
        name="mixed_parts",
        flops=4 * pairs * rows * width * hidden,
        after=after,
    )(ids, x, down_weight, down_weight)


def item_part(ids, d_gate, d_up, gate_weight, up_weight, width, after):
    rows, hidden = d_gate.shape
    shards = ids.shape[0]
    tile = tile_of(width, 512)
    steps = width // tile

    def kernel(ids_ref, dg, du, *refs):
        for i in range(shards):
            total = lax.dot_general(dg[...], refs[2 * i][...], NT, preferred_element_type=f32)
            total = total + lax.dot_general(du[...], refs[2 * i + 1][...], NT, preferred_element_type=f32)
            refs[2 * shards + i][0] = total.astype(bf16)

    whole = pl.BlockSpec((rows, hidden), lambda t, ids: (0, 0))
    specs = [whole, whole]
    for i in range(shards):
        specs += [pl.BlockSpec((tile, hidden), lambda t, ids, i=i: (ids[i] * steps + t, 0))] * 2
    return ordered_call(
        kernel,
        prefetch=1,
        grid=(steps,),
        in_specs=specs,
        out_specs=[pl.BlockSpec((1, rows, tile), lambda t, ids: (0, 0, t))] * shards,
        out_shape=[jax.ShapeDtypeStruct((1, rows, width), bf16)] * shards,
        name="item_part",
        flops=4 * shards * rows * width * hidden,
        after=after,
    )(ids, d_gate, d_up, *([gate_weight, up_weight] * shards))


def copy_chosen(index, options, after):
    rows, width = options[0].shape
    half = rows // 2

    def kernel(index_ref, *refs):
        for i in range(len(options)):

            @pl.when(index_ref[0] == i)
            def _():
                refs[-1][...] = refs[i][...]

    def block(i):
        return pl.BlockSpec((half, width), lambda t, index: (jnp.where(index[0] == i, t, 0), 0))

    return ordered_call(
        kernel,
        prefetch=1,
        grid=(2,),
        in_specs=[block(i) for i in range(len(options))],
        out_specs=[pl.BlockSpec((half, width), lambda t, index: (t, 0))],
        out_shape=[jax.ShapeDtypeStruct((rows, width), bf16)],
        name="copy_chosen",
        after=after,
    )(index, *options)


def copy_both(arrays, after):
    rows, width = arrays[0].shape
    many = len(arrays)

    def kernel(*refs):
        for i in range(many):
            refs[many + i][...] = refs[i][...]

    block = pl.BlockSpec((rows // 2, width), lambda t: (t, 0))
    return ordered_call(
        kernel,
        grid=(2,),
        in_specs=[block] * many,
        out_specs=[block] * many,
        out_shape=[jax.ShapeDtypeStruct(x.shape, x.dtype) for x in arrays],
        name="copy_both",
        after=after,
    )(*arrays)


def copy_small(arrays, after):
    many = len(arrays)

    def kernel(*refs):
        for i in range(many):
            refs[many + i][...] = refs[i][...]

    block = pl.BlockSpec(arrays[0].shape, lambda t: (0,) * arrays[0].ndim)
    return ordered_call(
        kernel,
        grid=(1,),
        in_specs=[block] * many,
        out_specs=[block] * many,
        out_shape=[jax.ShapeDtypeStruct(x.shape, x.dtype) for x in arrays],
        name="copy_small",
        after=after,
    )(*arrays)


def line_sums(wanted, parts, received, extra, after, flops=1 << 27):
    rows, width = parts[0][0].shape[1:]
    half = rows // 2
    outs = len(received)
    arrays = [x for pair in parts for x in pair]
    others = [x for group in received for x in group] + extra

    def kernel(wanted_ref, *refs):
        step = 0
        ins = refs[: outs * len(arrays)]
        adds = list(refs[outs * len(arrays) : -outs])
        for k in range(outs):
            terms = [adds.pop(0)[...].astype(f32) for _ in received[k]]
            terms += [x[...] for x in adds[len(adds) - len(extra) :]] if k == outs - 1 else []

            for i in range(len(parts)):

                @pl.when(wanted_ref[2 * k] == i)
                def _():
                    mine, theirs = ins[step + 2 * i], ins[step + 2 * i + 1]
                    total = functools.reduce(jnp.add, terms, mine[0].astype(f32) + theirs[0].astype(f32))
                    refs[len(refs) - outs + k][...] = total.astype(bf16)

            step += len(arrays)

    def block(k, i):
        def where(t, wanted):
            hit = wanted[2 * k] == i // 2
            return (jnp.where(hit, wanted[2 * k + 1], 0), jnp.where(hit, t, 0), 0)

        return pl.BlockSpec((1, half, width), where)

    flat = pl.BlockSpec((half, width), lambda t, wanted: (t, 0))
    return ordered_call(
        kernel,
        prefetch=1,
        grid=(2,),
        in_specs=[block(k, i) for k in range(outs) for i in range(len(arrays))] + [flat] * len(others),
        out_specs=[flat] * outs,
        out_shape=[jax.ShapeDtypeStruct((rows, width), bf16)] * outs,
        name="line_sums",
        flops=flops,
        after=after,
    )(wanted, *arrays * outs, *others)


def sum_small(arrays, after):
    def kernel(*refs):
        refs[-1][...] = functools.reduce(jnp.add, [x[...] for x in refs[:-1]])

    block = pl.BlockSpec(arrays[0].shape, lambda t: (0, 0))
    return ordered_call(
        kernel,
        grid=(1,),
        in_specs=[block] * len(arrays),
        out_specs=[block],
        out_shape=[jax.ShapeDtypeStruct(arrays[0].shape, f32)],
        name="sum_small",
        after=after,
    )(*arrays)


def low_rank(tokens, factor, after):
    rows, width = tokens.shape
    count, rank = factor.shape[:2]

    def kernel(x_ref, a_ref, o_ref):
        for i, part in enumerate(adapter_rows(count)):
            o_ref[part] = lax.dot_general(x_ref[part], a_ref[i], NT, preferred_element_type=f32)

    return ordered_call(
        kernel,
        grid=(1,),
        in_specs=[
            pl.BlockSpec((rows, width), lambda t: (0, 0)),
            pl.BlockSpec(factor.shape, lambda t: (0, 0, 0)),
        ],
        out_specs=[pl.BlockSpec((rows, rank), lambda t: (0, 0))],
        out_shape=[jax.ShapeDtypeStruct((rows, rank), f32)],
        name="low_rank",
        after=after,
    )(tokens, factor)


def low_rank_gradients(fill, lows, tokens, factor, after):
    rows, width = tokens.shape
    count, rank = factor.shape[:2]

    def kernel(fill_ref, x_ref, a_ref, *refs):
        d_low = functools.reduce(jnp.add, [x[...] for x in refs[:-2]])
        for i, part in enumerate(adapter_rows(count)):
            alive = lax.broadcasted_iota(jnp.int32, (BLOCK, rank), 0) < fill_ref[i]
            d = jnp.where(alive, adapter_scale * d_low[part], 0.0).astype(bf16)
            grad = lax.dot_general(d, x_ref[part], (((0,), (0,)), ((), ())), preferred_element_type=f32)
            refs[-2][i] = grad.astype(bf16)
            refs[-1][part] = jnp.dot(d, a_ref[i], preferred_element_type=f32)

    block = pl.BlockSpec(factor.shape, lambda t, fill: (0, 0, 0))
    whole = pl.BlockSpec((rows, width), lambda t, fill: (0, 0))
    return ordered_call(
        kernel,
        prefetch=1,
        grid=(1,),
        in_specs=[whole, block] + [pl.BlockSpec((rows, rank), lambda t, fill: (0, 0))] * len(lows),
        out_specs=[block, whole],
        out_shape=[jax.ShapeDtypeStruct(factor.shape, bf16), jax.ShapeDtypeStruct((rows, width), f32)],
        name="low_rank_gradients",
        flops=COVER,
        after=after,
    )(fill, tokens, factor, *lows)


def pick_slots(places, in_factor, out_factor, after):
    many = places.shape[0]

    def kernel(places_ref, a_ref, b_ref, oa, ob):
        held = places_ref[pl.program_id(0)] >= 0

        @pl.when(held)
        def _():
            oa[...] = a_ref[...]
            ob[...] = b_ref[...]

        @pl.when(~held)
        def _():
            oa[...] = jnp.zeros_like(oa)
            ob[...] = jnp.zeros_like(ob)

    def block(factor):
        return (1,) + factor.shape[1:]

    picked = [pl.BlockSpec(block(f), lambda i, ids: (jnp.maximum(ids[i], 0), 0, 0)) for f in (in_factor, out_factor)]
    out = [pl.BlockSpec(block(f), lambda i, ids: (i, 0, 0)) for f in (in_factor, out_factor)]
    return ordered_call(
        kernel,
        prefetch=1,
        grid=(many,),
        in_specs=picked,
        out_specs=out,
        out_shape=[jax.ShapeDtypeStruct((many,) + f.shape[1:], bf16) for f in (in_factor, out_factor)],
        name="pick_slots",
        after=after,
    )(places, in_factor, out_factor)


def slot_sums(places, grads, slots, after, flops=1 << 27):
    total_blocks, rank, width = grads.shape

    def kernel(places_ref, *rest):
        ins, out, total = rest
        out[...] = jnp.zeros_like(out)
        for i in range(total_blocks):
            place = places_ref[i]
            earlier = functools.reduce(jnp.logical_or, [places_ref[j] == place for j in range(i)], False)
            later = functools.reduce(jnp.logical_or, [places_ref[j] == place for j in range(i + 1, total_blocks)], False)
            here = ins.at[i]
            held = place >= 0

            @pl.when(held & ~jnp.logical_or(earlier, later))
            def _():
                out[pl.ds(jnp.maximum(place, 0), 1)] = here[...][None]

            @pl.when(held & ~jnp.asarray(earlier) & later)
            def _():
                total[...] = here[...].astype(f32)
                for j in range(i + 1, total_blocks):

                    @pl.when(places_ref[j] == place)
                    def _():
                        total[...] += ins[j].astype(f32)

                out[pl.ds(jnp.maximum(place, 0), 1)] = total[...].astype(bf16)[None]

    return ordered_call(
        kernel,
        prefetch=1,
        grid=(1,),
        in_specs=[pl.BlockSpec((total_blocks, rank, width), lambda s, ids: (0, 0, 0))],
        out_specs=[pl.BlockSpec((slots, rank, width), lambda s, ids: (0, 0, 0))],
        scratch=[pltpu.VMEM((rank, width), f32)],
        out_shape=[jax.ShapeDtypeStruct((slots, rank, width), bf16)],
        name="slot_sums",
        flops=flops,
        after=after,
    )(places, grads)


def line_pairs(sources, step):
    return [(2 * z + core, 2 * (z + step) + core) for z in sources for core in (0, 1)]


def swap_cores(x, chips):
    return lax.ppermute(x, "tensor", [(i, i ^ 1) for i in range(2 * chips)])


def arrival_order(chips):
    order = []
    for z in range(chips):
        up, down = list(range(z + 1, chips)), list(range(z - 1, -1, -1))
        order.append([z] + (up + down if 2 * z < chips else down + up))
    return order


def line_hop(left, right, s, chips):
    return [
        lax.ppermute(left, "tensor", line_pairs(range(s - 1, chips - 1), 1)),
        lax.ppermute(right, "tensor", line_pairs(range(1, chips - s + 1), -1)),
    ]


def last_hop(shard, chips):
    both = lax.ppermute(shard, "tensor", line_pairs([chips - 2], 1) + line_pairs([1], -1))
    return [both, both]


def stage_shard(chip, left, right, j, chips, after):
    options, where = [], []
    for z, row in enumerate(arrival_order(chips)):
        value = left[z - row[j]] if row[j] <= z else right[row[j] - z]
        spot = next((i for i, option in enumerate(options) if option is value), len(options))
        if spot == len(options):
            options.append(value)
        where.append(spot)
    return copy_chosen(jnp.array(where, jnp.int32)[chip][None], options, after)


def send_order(chips):
    order = []
    for z in range(chips):
        due = []
        for s in range(1, chips):
            if z <= s - 1:
                due.append(chips - s + z)
            if z >= chips - s:
                due.append(s - chips + z)
        order.append(due + [z])
    return order


def scatter_sums(chip, parts, received, s, chips, after):
    stage = [{d: j for j, d in enumerate(row)} for row in send_order(chips)]
    entries = [(i, k) for i, pair in enumerate(parts) for k in range(pair[0].shape[0])]

    def named(table):
        return jnp.array(table, jnp.int32)[chip]

    if s == 1:
        wanted = named([entries[0]] * chips)
        return line_sums(wanted, parts[:1], [[]], [], after)
    up = [entries[stage[z][chips - s + z]] if z <= s - 1 else entries[0] for z in range(chips)]
    down = [entries[stage[z][s - chips + z]] if z >= chips - s else entries[0] for z in range(chips)]
    wanted = named([list(a) + list(b) for a, b in zip(up, down)])
    return line_sums(wanted, parts, [[received[0]], [received[1]]], [], after)


def scatter_hop(payload, s, chips):
    up, down = line_pairs(range(0, s), 1), line_pairs(range(chips - s, chips), -1)
    if len(payload) == 1:
        both = lax.ppermute(payload[0], "tensor", up + down)
        return [both, both]
    return [lax.ppermute(payload[0], "tensor", up), lax.ppermute(payload[1], "tensor", down)]


def scatter_end(part, received, extra, after):
    entry = part[0].shape[0] - 1
    return line_sums(jnp.array([0, entry], jnp.int32), [part], [list(received)], extra, after)


def body(
    tokens,
    cotangent,
    gate_weight,
    up_weight,
    down_weight,
    block_task,
    block_fill,
    task_slot,
    inner_correction_weights,
    up_b,
):
    size, groups = lax.axis_size("tensor"), lax.axis_size("dp")
    chips = size // 2
    last, half = chips - 1, chips // 2
    me, group = lax.axis_index("tensor"), lax.axis_index("dp")
    chip, core = me // 2, me % 2
    rows, width = tokens.shape
    count = block_task.shape[0]
    slots, rank = inner_correction_weights.shape[:2]
    distances = [1 << i for i in range(size.bit_length() - 1)]

    def exchange(x, r):
        return lax.ppermute(x, "dp", [(d, d ^ r) for d in range(groups)])

    def from_distance(x, distance):
        return lax.ppermute(x, "tensor", [(i, i ^ distance) for i in range(size)])

    def pairs(table):
        return jnp.stack([2 * table + core, 2 * table + 1 - core], axis=1).reshape(-1).astype(jnp.int32)

    order = pairs(jnp.array(arrival_order(chips), jnp.int32)[chip])
    targets = pairs(jnp.array(send_order(chips), jnp.int32)[chip])

    hop = line_hop(tokens, tokens, 1, chips)
    shards = [tokens, swap_cores(tokens, chips)]
    task_ids = jnp.arange(task_slot.shape[0], dtype=jnp.int32)
    slot = jnp.sum(jnp.where(block_task[:, None] == task_ids[None, :], task_slot[None, :], 0), axis=1)
    wanted, bit = slot, 1
    while bit < groups:
        theirs = exchange(wanted, bit)
        low_side = (group & bit) == 0
        wanted = jnp.concatenate([jnp.where(low_side, wanted, theirs), jnp.where(low_side, theirs, wanted)])
        bit *= 2
    place = wanted - group * slots
    places = jnp.where(jnp.logical_and(place >= 0, place < slots), place, -1)

    left, right, sums, mark = [tokens], [tokens], [], None
    begun = 0
    for j in range(1, chips):
        left.append(hop[0])
        right.append(hop[1])
        if j < last - 1:
            hop = line_hop(left[j], right[j], j + 1, chips)
        mine, mark = stage_shard(chip, left, right, j, chips, [mark] if j > 1 else [])
        if j == 1:
            picked_in, picked_out, mark = pick_slots(places, inner_correction_weights, up_b, [mark])
            factor_in = lax.psum_scatter(picked_in, "dp", scatter_dimension=0, tiled=True)
            factor_out = lax.psum_scatter(picked_out, "dp", scatter_dimension=0, tiled=True)
        if j == last - 1:
            hop = last_hop(mine, chips)
        shards += [mine, swap_cores(mine, chips)]
        if j in (half - 1, last - 1):
            *sums, mark = forward_part(
                order[2 * begun : 2 * j + 2], shards, gate_weight, up_weight, sums, [mark]
            )
            shards, begun = [], j + 1
        if j == last - 1:
            low, mark = low_rank(tokens, factor_in, [mark])
            low, mark = sum_small([low, from_distance(low, 1)], [mark])
            cotangent, mark = copy_both([cotangent], [mark])
    far = [from_distance(low, 2 * k) for k in range(1, chips)]
    cotangent_hop = line_hop(cotangent, cotangent, 1, chips)
    cotangent_other = swap_cores(cotangent, chips)
    gate, up, mark = forward_part(order[2 * begun :], shards, gate_weight, up_weight, sums, [mark])
    low = sum_small([low] + far, [mark])[0]
    live = (jnp.arange(BLOCK, dtype=jnp.int32)[None, :] < block_fill[:, None]).astype(f32)[..., None]
    low_b = (low.reshape(count, BLOCK, rank) * live).astype(bf16).reshape(rows, rank)
    left, right = [cotangent], [cotangent]
    hidden_b, act, slope, mark = activate(gate, up, low_b, factor_out, [mark])
    first = copy_both(cotangent_hop, [mark])
    left.append(first[0])
    right.append(first[1])
    cotangent_hop = line_hop(left[1], right[1], 2, chips)

    def mixed_part(which, after):
        mine, theirs, mark = mixed_parts(targets[which], hidden_b, down_weight, width, after)
        return (mine, swap_cores(theirs, chips)), mark

    mixed = []
    part, mark = mixed_part(slice(0, 2), [first[-1]])
    mixed.append(part)
    part, mark = mixed_part(slice(2, 2 * chips), [mark])
    mixed.append(part)
    shards = [cotangent, cotangent_other]
    for j in range(1, chips):
        if j > 1:
            left.append(cotangent_hop[0])
            right.append(cotangent_hop[1])
            if j < last - 1:
                cotangent_hop = line_hop(left[j], right[j], j + 1, chips)
        value, mark = stage_shard(chip, left, right, j, chips, [mark])
        if j == last - 1:
            cotangent_hop = last_hop(value, chips)
            *payload, mark = scatter_sums(chip, mixed, None, 1, chips, [mark])
            mixed_hop = scatter_hop(payload, 1, chips)
            total, mark = hidden_part(order[: 2 * half], shards[: 2 * half], down_weight, [mark])
        shards += [value, swap_cores(value, chips)]
    *payload, mark = scatter_sums(chip, mixed, mixed_hop, 2, chips, [mark])
    mixed_hop = scatter_hop(payload, 2, chips)
    d_gate, d_up, d_low, out_grad, mark = hidden_gradients(
        order[2 * half :], shards[2 * half :], down_weight, total, act, slope, low_b, factor_out, [mark]
    )

    def item(which, after):
        return item_part(targets[which], d_gate, d_up, gate_weight, up_weight, width, after)

    out_grads = lax.all_gather(out_grad, "dp", axis=0, tiled=True)
    near_low = from_distance(d_low, distances[0])
    for s in range(3, chips):
        *payload, mark = scatter_sums(chip, mixed, mixed_hop, s, chips, [mark])
        mixed_hop = scatter_hop(payload, s, chips)
    theirs, mark = item(slice(1, 2), [mark])
    theirs = swap_cores(theirs, chips)
    d_low, mark = sum_small([d_low, near_low], [mark])
    far_low = from_distance(d_low, distances[1])
    mine, mark = item(slice(0, 1), [mark])
    parts = [(mine, theirs)]
    for distance in distances[2:]:
        d_low, mark = sum_small([d_low, far_low], [mark])
        far_low = from_distance(d_low, distance)
    item_hop = None
    bits = [1 << i for i in range(groups.bit_length() - 1)]
    for j in range(1, chips):
        *payload, mark = scatter_sums(chip, parts, item_hop, j, chips, [mark])
        item_hop = scatter_hop(payload, j, chips)
        mine, theirs, mark = item(slice(2 * j, 2 * j + 2), [mark])
        parts.append((mine, swap_cores(theirs, chips)))
        if j == 1:
            in_grad, through, mark = low_rank_gradients(
                block_fill, [d_low, far_low], tokens, factor_in, [mark]
            )
            in_grads = {0: in_grad} | {bit: exchange(in_grad, bit) for bit in bits}
            mixed, mark = scatter_end(mixed[-1], mixed_hop, [], [mark])
        if j == 2:
            out_sums, mark = slot_sums(places, out_grads, slots, [mark])
            near = copy_small([in_grads[bit] for bit in bits], [mark])
            mark = near[-1]
            in_grads |= dict(zip(bits, near))
            for r in range(1, groups):
                if r not in in_grads:
                    top = 1 << (r.bit_length() - 1)
                    in_grads[r] = exchange(in_grads[top], r ^ top)
    near_places = jnp.concatenate(
        [lax.dynamic_slice_in_dim(places, (group ^ r) * count, count, 0) for r in range(groups)]
    )
    in_grads = jnp.concatenate([in_grads[r] for r in range(groups)])
    in_sums, mark = slot_sums(near_places, in_grads, slots, [mark], flops=COVER)
    item_derivative = scatter_end(parts[-1], item_hop, [through], [mark])[0]
    return (mixed, item_derivative, in_sums, out_sums)


def solution(mesh):
    return jax.shard_map(
        body,
        mesh=mesh,
        in_specs=(
            P("dp", "tensor"),
            P("dp", "tensor"),
            P(None, "tensor"),
            P(None, "tensor"),
            P("tensor", None),
            P("dp"),
            P("dp"),
            P(),
            P("dp", None, "tensor"),
            P("dp", None, "tensor"),
        ),
        out_specs=(
            P("dp", "tensor"),
            P("dp", "tensor"),
            P("dp", None, "tensor"),
            P("dp", None, "tensor"),
        ),
        check_vma=False,
    )
```

```python
import functools

import jax
import jax.numpy as jnp
from jax import lax
from jax.experimental import pallas as pl
from jax.experimental.pallas import tpu as pltpu
from jax.sharding import PartitionSpec as P

BLOCK = 128
adapter_scale = 0.25
VMEM_LIMIT = 32 * 1024 * 1024
COVER = 1 << 32
f32 = jnp.float32
bf16 = jnp.bfloat16
NT = (((1,), (1,)), ((), ()))


def params():
    return pltpu.CompilerParams(vmem_limit_bytes=VMEM_LIMIT)


def tile_of(size, most=256):
    return next((t for t in range(most, 127, -128) if size % t == 0), size)


def ordered_call(kernel, *, grid, in_specs, out_specs, out_shape, name, flops=1 << 27, prefetch=0, scratch=(), after=(), far=None):
    many = prefetch + len(in_specs)
    outs = len(out_specs)

    def run(*refs):
        mark = refs[many + len(after) + outs]
        mark[...] = jnp.zeros_like(mark)
        kernel(*refs[:many], *refs[many + len(after) : many + len(after) + outs], *refs[many + len(after) + outs + 1 :])

    def shape_of(x):
        return pltpu.HBM(x.shape, x.dtype) if x.shape == far else x

    call = pl.pallas_call(
        run,
        grid_spec=pltpu.PrefetchScalarGridSpec(
            num_scalar_prefetch=prefetch,
            grid=grid,
            in_specs=list(in_specs) + [pl.BlockSpec(memory_space=pl.ANY)] * len(after),
            out_specs=list(out_specs) + [pl.BlockSpec((8, 128), lambda *_: (0, 0))],
            scratch_shapes=list(scratch),
        ),
        out_shape=[shape_of(x) if x.dtype == f32 else x for x in out_shape] + [jax.ShapeDtypeStruct((8, 128), f32)],
        compiler_params=params(),
        cost_estimate=pl.CostEstimate(flops=flops, bytes_accessed=flops // 384, transcendentals=0),
        name=name,
    )
    def place(x):
        hold = x.shape == far and x.dtype == f32 and name != "activate"
        return pltpu.with_memory_space_constraint(x, pltpu.HBM) if hold else x

    return lambda *operands: call(*(place(x) for x in operands), *after)


def adapter_rows(count):
    return [slice(i * BLOCK, (i + 1) * BLOCK) for i in range(count)]


def forward_part(ids, shards, gate_weight, up_weight, sums, after):
    rows, width = shards[0].shape
    hidden = gate_weight.shape[1]
    tile = tile_of(hidden)
    many = len(shards)

    def kernel(ids_ref, *refs):
        xs, gs, us = refs[:many], refs[many : 2 * many], refs[2 * many : 3 * many]
        g = u = None
        if sums:
            g, u = refs[3 * many][...], refs[3 * many + 1][...]
        for x, wg, wu in zip(xs, gs, us):
            a = x[...]
            pg = jnp.dot(a, wg[...], preferred_element_type=f32)
            pu = jnp.dot(a, wu[...], preferred_element_type=f32)
            g, u = (pg, pu) if g is None else (g + pg, u + pu)
        refs[-2][...] = g
        refs[-1][...] = u

    whole = pl.BlockSpec((rows, width), lambda t, ids: (0, 0))
    weights = [pl.BlockSpec((width, tile), lambda t, ids, i=i: (ids[i], t)) for i in range(many)]
    acc = pl.BlockSpec((rows, tile), lambda t, ids: (0, t))
    shape = jax.ShapeDtypeStruct((rows, hidden), f32)
    return ordered_call(
        kernel,
        prefetch=1,
        grid=(hidden // tile,),
        in_specs=[whole] * many + weights + weights + [acc] * len(sums),
        out_specs=[acc, acc],
        out_shape=[shape, shape],
        name="forward_part",
        flops=4 * many * rows * width * hidden,
        after=after,
    )(ids, *shards, *[gate_weight] * many, *[up_weight] * many, *sums)


def activate(gate, up, low_b, factor, after):
    rows, hidden = gate.shape
    tile = tile_of(hidden, 512)
    count, rank = factor.shape[0], factor.shape[1]

    def kernel(g_ref, u_ref, low_ref, b_ref, h_ref, act_ref, slope_ref):
        for i, part in enumerate(adapter_rows(count)):
            g = g_ref[part]
            u = u_ref[part] + adapter_scale * jnp.dot(low_ref[part], b_ref[i], preferred_element_type=f32)
            s = jax.nn.sigmoid(g)
            act = g * s
            act_ref[part] = act
            h_ref[part] = (act * u).astype(bf16)
            slope_ref[part] = u * s * (1.0 + g * (1.0 - s))

    acc = pl.BlockSpec((rows, tile), lambda t: (0, t))
    return ordered_call(
        kernel,
        grid=(hidden // tile,),
        in_specs=[
            acc, acc,
            pl.BlockSpec((rows, rank), lambda t: (0, 0)),
            pl.BlockSpec((count, rank, tile), lambda t: (0, 0, t)),
        ],
        out_specs=[acc, acc, acc],
        out_shape=[
            jax.ShapeDtypeStruct((rows, hidden), bf16),
            jax.ShapeDtypeStruct((rows, hidden), f32),
            jax.ShapeDtypeStruct((rows, hidden), f32),
        ],
        name="activate",
        far=(rows, hidden),
        flops=1 << 31,
        after=after,
    )(gate, up, low_b, factor)


def hidden_product(x_refs, w_refs):
    return functools.reduce(
        jnp.add,
        [lax.dot_general(x[...], w[...], NT, preferred_element_type=f32) for x, w in zip(x_refs, w_refs)],
    )


def hidden_part(ids, shards, down_weight, after):
    rows, width = shards[0].shape
    hidden = down_weight.shape[0]
    tile = tile_of(hidden)
    many = len(shards)

    def kernel(ids_ref, *refs):
        refs[-1][...] = hidden_product(refs[:many], refs[many:-1])

    whole = pl.BlockSpec((rows, width), lambda t, ids: (0, 0))
    weights = [pl.BlockSpec((tile, width), lambda t, ids, i=i: (t, ids[i])) for i in range(many)]
    return ordered_call(
        kernel,
        prefetch=1,
        grid=(hidden // tile,),
        in_specs=[whole] * many + weights,
        out_specs=[pl.BlockSpec((rows, tile), lambda t, ids: (0, t))],
        out_shape=[jax.ShapeDtypeStruct((rows, hidden), f32)],
        name="hidden_part",
        far=(rows, hidden),
        flops=2 * many * rows * width * hidden,
        after=after,
    )(ids, *shards, *([down_weight] * many))


def hidden_gradients(ids, shards, down_weight, total, act, slope, low_b, factor, after):
    rows, width = shards[0].shape
    hidden = down_weight.shape[0]
    tile = tile_of(hidden)
    count, rank = factor.shape[0], factor.shape[1]
    many = len(shards)

    def kernel(ids_ref, *refs):
        d_ref, act_ref, slope_ref, low_ref, b_ref, dg_ref, du_ref, dl_ref, gb_ref = refs[2 * many :]
        d = d_ref[...] + hidden_product(refs[:many], refs[many : 2 * many])
        dg_ref[...] = (d * slope_ref[...]).astype(bf16)
        du = (d * act_ref[...]).astype(bf16)
        du_ref[...] = du

        @pl.when(pl.program_id(0) == 0)
        def _():
            dl_ref[...] = jnp.zeros_like(dl_ref)

        for i, part in enumerate(adapter_rows(count)):
            dl_ref[part] += lax.dot_general(du[part], b_ref[i], NT, preferred_element_type=f32)
            grad = lax.dot_general(low_ref[part], du[part], (((0,), (0,)), ((), ())), preferred_element_type=f32)
            gb_ref[i] = (adapter_scale * grad).astype(bf16)

    whole = pl.BlockSpec((rows, width), lambda t, ids: (0, 0))
    weights = [pl.BlockSpec((tile, width), lambda t, ids, i=i: (t, ids[i])) for i in range(many)]
    acc = pl.BlockSpec((rows, tile), lambda t, ids: (0, t))
    lows = pl.BlockSpec((rows, rank), lambda t, ids: (0, 0))
    factors = pl.BlockSpec((count, rank, tile), lambda t, ids: (0, 0, t))
    return ordered_call(
        kernel,
        prefetch=1,
        grid=(hidden // tile,),
        in_specs=[whole] * many + weights + [acc, acc, acc, lows, factors],
        out_specs=[acc, acc, lows, factors],
        out_shape=[
            jax.ShapeDtypeStruct((rows, hidden), bf16),
            jax.ShapeDtypeStruct((rows, hidden), bf16),
            jax.ShapeDtypeStruct((rows, rank), f32),
            jax.ShapeDtypeStruct((count, rank, hidden), bf16),
        ],
        name="hidden_gradients",
        far=(rows, hidden),
        flops=2 * many * rows * width * hidden,
        after=after,
    )(ids, *shards, *([down_weight] * many), total, act, slope, low_b, factor)


def mixed_parts(ids, x, down_weight, width, after):
    rows, hidden = x.shape
    tile = tile_of(width, 512)
    steps = width // tile
    pairs = ids.shape[0] // 2

    def kernel(ids_ref, x_ref, wa, wb, oa, ob):
        oa[0] = jnp.dot(x_ref[...], wa[...], preferred_element_type=f32).astype(bf16)
        ob[0] = jnp.dot(x_ref[...], wb[...], preferred_element_type=f32).astype(bf16)

    out = pl.BlockSpec((1, rows, tile), lambda j, t, ids: (j, 0, t))
    shape = jax.ShapeDtypeStruct((pairs, rows, width), bf16)
    return ordered_call(
        kernel,
        prefetch=1,
        grid=(pairs, steps),
        in_specs=[
            pl.BlockSpec((rows, hidden), lambda j, t, ids: (0, 0)),
            pl.BlockSpec((hidden, tile), lambda j, t, ids: (0, ids[2 * j] * steps + t)),
            pl.BlockSpec((hidden, tile), lambda j, t, ids: (0, ids[2 * j + 1] * steps + t)),
        ],
        out_specs=[out, out],
        out_shape=[shape, shape],
        name="mixed_parts",
        flops=4 * pairs * rows * width * hidden,
        after=after,
    )(ids, x, down_weight, down_weight)


def item_part(ids, d_gate, d_up, gate_weight, up_weight, width, after):
    rows, hidden = d_gate.shape
    shards = ids.shape[0]
    tile = tile_of(width, 512)
    steps = width // tile

    def kernel(ids_ref, dg, du, *refs):
        for i in range(shards):
            total = lax.dot_general(dg[...], refs[2 * i][...], NT, preferred_element_type=f32)
            total = total + lax.dot_general(du[...], refs[2 * i + 1][...], NT, preferred_element_type=f32)
            refs[2 * shards + i][0] = total.astype(bf16)

    whole = pl.BlockSpec((rows, hidden), lambda t, ids: (0, 0))
    specs = [whole, whole]
    for i in range(shards):
        specs += [pl.BlockSpec((tile, hidden), lambda t, ids, i=i: (ids[i] * steps + t, 0))] * 2
    return ordered_call(
        kernel,
        prefetch=1,
        grid=(steps,),
        in_specs=specs,
        out_specs=[pl.BlockSpec((1, rows, tile), lambda t, ids: (0, 0, t))] * shards,
        out_shape=[jax.ShapeDtypeStruct((1, rows, width), bf16)] * shards,
        name="item_part",
        flops=4 * shards * rows * width * hidden,
        after=after,
    )(ids, d_gate, d_up, *([gate_weight, up_weight] * shards))


def copy_chosen(index, options, after):
    rows, width = options[0].shape
    half = rows // 2

    def kernel(index_ref, *refs):
        for i in range(len(options)):

            @pl.when(index_ref[0] == i)
            def _():
                refs[-1][...] = refs[i][...]

    def block(i):
        return pl.BlockSpec((half, width), lambda t, index: (jnp.where(index[0] == i, t, 0), 0))

    return ordered_call(
        kernel,
        prefetch=1,
        grid=(2,),
        in_specs=[block(i) for i in range(len(options))],
        out_specs=[pl.BlockSpec((half, width), lambda t, index: (t, 0))],
        out_shape=[jax.ShapeDtypeStruct((rows, width), bf16)],
        name="copy_chosen",
        after=after,
    )(index, *options)


def copy_both(arrays, after):
    rows, width = arrays[0].shape
    many = len(arrays)

    def kernel(*refs):
        for i in range(many):
            refs[many + i][...] = refs[i][...]

    block = pl.BlockSpec((rows // 2, width), lambda t: (t, 0))
    return ordered_call(
        kernel,
        grid=(2,),
        in_specs=[block] * many,
        out_specs=[block] * many,
        out_shape=[jax.ShapeDtypeStruct(x.shape, x.dtype) for x in arrays],
        name="copy_both",
        after=after,
    )(*arrays)


def copy_small(arrays, after):
    many = len(arrays)

    def kernel(*refs):
        for i in range(many):
            refs[many + i][...] = refs[i][...]

    block = pl.BlockSpec(arrays[0].shape, lambda t: (0,) * arrays[0].ndim)
    return ordered_call(
        kernel,
        grid=(1,),
        in_specs=[block] * many,
        out_specs=[block] * many,
        out_shape=[jax.ShapeDtypeStruct(x.shape, x.dtype) for x in arrays],
        name="copy_small",
        after=after,
    )(*arrays)


def line_sums(wanted, parts, received, extra, after, flops=1 << 27):
    rows, width = parts[0][0].shape[1:]
    half = rows // 2
    outs = len(received)
    arrays = [x for pair in parts for x in pair]
    others = [x for group in received for x in group] + extra

    def kernel(wanted_ref, *refs):
        step = 0
        ins = refs[: outs * len(arrays)]
        adds = list(refs[outs * len(arrays) : -outs])
        for k in range(outs):
            terms = [adds.pop(0)[...].astype(f32) for _ in received[k]]
            terms += [x[...] for x in adds[len(adds) - len(extra) :]] if k == outs - 1 else []

            for i in range(len(parts)):

                @pl.when(wanted_ref[2 * k] == i)
                def _():
                    mine, theirs = ins[step + 2 * i], ins[step + 2 * i + 1]
                    total = functools.reduce(jnp.add, terms, mine[0].astype(f32) + theirs[0].astype(f32))
                    refs[len(refs) - outs + k][...] = total.astype(bf16)

            step += len(arrays)

    def block(k, i):
        def where(t, wanted):
            hit = wanted[2 * k] == i // 2
            return (jnp.where(hit, wanted[2 * k + 1], 0), jnp.where(hit, t, 0), 0)

        return pl.BlockSpec((1, half, width), where)

    flat = pl.BlockSpec((half, width), lambda t, wanted: (t, 0))
    return ordered_call(
        kernel,
        prefetch=1,
        grid=(2,),
        in_specs=[block(k, i) for k in range(outs) for i in range(len(arrays))] + [flat] * len(others),
        out_specs=[flat] * outs,
        out_shape=[jax.ShapeDtypeStruct((rows, width), bf16)] * outs,
        name="line_sums",
        flops=flops,
        after=after,
    )(wanted, *arrays * outs, *others)


def sum_small(arrays, after):
    def kernel(*refs):
        refs[-1][...] = functools.reduce(jnp.add, [x[...] for x in refs[:-1]])

    block = pl.BlockSpec(arrays[0].shape, lambda t: (0, 0))
    return ordered_call(
        kernel,
        grid=(1,),
        in_specs=[block] * len(arrays),
        out_specs=[block],
        out_shape=[jax.ShapeDtypeStruct(arrays[0].shape, f32)],
        name="sum_small",
        after=after,
    )(*arrays)


def low_rank(tokens, factor, after):
    rows, width = tokens.shape
    count, rank = factor.shape[:2]

    def kernel(x_ref, a_ref, o_ref):
        for i, part in enumerate(adapter_rows(count)):
            o_ref[part] = lax.dot_general(x_ref[part], a_ref[i], NT, preferred_element_type=f32)

    return ordered_call(
        kernel,
        grid=(1,),
        in_specs=[
            pl.BlockSpec((rows, width), lambda t: (0, 0)),
            pl.BlockSpec(factor.shape, lambda t: (0, 0, 0)),
        ],
        out_specs=[pl.BlockSpec((rows, rank), lambda t: (0, 0))],
        out_shape=[jax.ShapeDtypeStruct((rows, rank), f32)],
        name="low_rank",
        after=after,
    )(tokens, factor)


def low_rank_gradients(fill, lows, tokens, factor, after):
    rows, width = tokens.shape
    count, rank = factor.shape[:2]

    def kernel(fill_ref, x_ref, a_ref, *refs):
        d_low = functools.reduce(jnp.add, [x[...] for x in refs[:-2]])
        for i, part in enumerate(adapter_rows(count)):
            alive = lax.broadcasted_iota(jnp.int32, (BLOCK, rank), 0) < fill_ref[i]
            d = jnp.where(alive, adapter_scale * d_low[part], 0.0).astype(bf16)
            grad = lax.dot_general(d, x_ref[part], (((0,), (0,)), ((), ())), preferred_element_type=f32)
            refs[-2][i] = grad.astype(bf16)
            refs[-1][part] = jnp.dot(d, a_ref[i], preferred_element_type=f32)

    block = pl.BlockSpec(factor.shape, lambda t, fill: (0, 0, 0))
    whole = pl.BlockSpec((rows, width), lambda t, fill: (0, 0))
    return ordered_call(
        kernel,
        prefetch=1,
        grid=(1,),
        in_specs=[whole, block] + [pl.BlockSpec((rows, rank), lambda t, fill: (0, 0))] * len(lows),
        out_specs=[block, whole],
        out_shape=[jax.ShapeDtypeStruct(factor.shape, bf16), jax.ShapeDtypeStruct((rows, width), f32)],
        name="low_rank_gradients",
        after=after,
    )(fill, tokens, factor, *lows)


def pick_slots(places, in_factor, out_factor, after):
    many = places.shape[0]

    def kernel(places_ref, a_ref, b_ref, oa, ob):
        held = places_ref[pl.program_id(0)] >= 0

        @pl.when(held)
        def _():
            oa[...] = a_ref[...]
            ob[...] = b_ref[...]

        @pl.when(~held)
        def _():
            oa[...] = jnp.zeros_like(oa)
            ob[...] = jnp.zeros_like(ob)

    def block(factor):
        return (1,) + factor.shape[1:]

    picked = [pl.BlockSpec(block(f), lambda i, ids: (jnp.maximum(ids[i], 0), 0, 0)) for f in (in_factor, out_factor)]
    out = [pl.BlockSpec(block(f), lambda i, ids: (i, 0, 0)) for f in (in_factor, out_factor)]
    return ordered_call(
        kernel,
        prefetch=1,
        grid=(many,),
        in_specs=picked,
        out_specs=out,
        out_shape=[jax.ShapeDtypeStruct((many,) + f.shape[1:], bf16) for f in (in_factor, out_factor)],
        name="pick_slots",
        after=after,
    )(places, in_factor, out_factor)


def slot_sums(places, grads, slots, after, flops=1 << 27):
    total_blocks, rank, width = grads.shape

    def kernel(places_ref, *rest):
        ins, out, total = rest
        out[...] = jnp.zeros_like(out)
        for i in range(total_blocks):
            place = places_ref[i]
            earlier = functools.reduce(jnp.logical_or, [places_ref[j] == place for j in range(i)], False)
            later = functools.reduce(jnp.logical_or, [places_ref[j] == place for j in range(i + 1, total_blocks)], False)
            here = ins.at[i]
            held = place >= 0

            @pl.when(held & ~jnp.logical_or(earlier, later))
            def _():
                out[pl.ds(jnp.maximum(place, 0), 1)] = here[...][None]

            @pl.when(held & ~jnp.asarray(earlier) & later)
            def _():
                total[...] = here[...].astype(f32)
                for j in range(i + 1, total_blocks):

                    @pl.when(places_ref[j] == place)
                    def _():
                        total[...] += ins[j].astype(f32)

                out[pl.ds(jnp.maximum(place, 0), 1)] = total[...].astype(bf16)[None]

    return ordered_call(
        kernel,
        prefetch=1,
        grid=(1,),
        in_specs=[pl.BlockSpec((total_blocks, rank, width), lambda s, ids: (0, 0, 0))],
        out_specs=[pl.BlockSpec((slots, rank, width), lambda s, ids: (0, 0, 0))],
        scratch=[pltpu.VMEM((rank, width), f32)],
        out_shape=[jax.ShapeDtypeStruct((slots, rank, width), bf16)],
        name="slot_sums",
        flops=flops,
        after=after,
    )(places, grads)


def line_pairs(sources, step):
    return [(2 * z + core, 2 * (z + step) + core) for z in sources for core in (0, 1)]


def swap_cores(x, chips):
    return lax.ppermute(x, "tensor", [(i, i ^ 1) for i in range(2 * chips)])


def arrival_order(chips):
    order = []
    for z in range(chips):
        up, down = list(range(z + 1, chips)), list(range(z - 1, -1, -1))
        order.append([z] + (up + down if 2 * z < chips else down + up))
    return order


def line_hop(left, right, s, chips):
    return [
        lax.ppermute(left, "tensor", line_pairs(range(s - 1, chips - 1), 1)),
        lax.ppermute(right, "tensor", line_pairs(range(1, chips - s + 1), -1)),
    ]


def last_hop(shard, chips):
    both = lax.ppermute(shard, "tensor", line_pairs([chips - 2], 1) + line_pairs([1], -1))
    return [both, both]


def stage_shard(chip, left, right, j, chips, after):
    options, where = [], []
    for z, row in enumerate(arrival_order(chips)):
        value = left[z - row[j]] if row[j] <= z else right[row[j] - z]
        spot = next((i for i, option in enumerate(options) if option is value), len(options))
        if spot == len(options):
            options.append(value)
        where.append(spot)
    return copy_chosen(jnp.array(where, jnp.int32)[chip][None], options, after)


def send_order(chips):
    order = []
    for z in range(chips):
        due = []
        for s in range(1, chips):
            if z <= s - 1:
                due.append(chips - s + z)
            if z >= chips - s:
                due.append(s - chips + z)
        order.append(due + [z])
    return order


def scatter_sums(chip, parts, received, s, chips, after):
    stage = [{d: j for j, d in enumerate(row)} for row in send_order(chips)]
    entries = [(i, k) for i, pair in enumerate(parts) for k in range(pair[0].shape[0])]

    def named(table):
        return jnp.array(table, jnp.int32)[chip]

    if s == 1:
        wanted = named([entries[0]] * chips)
        return line_sums(wanted, parts[:1], [[]], [], after)
    up = [entries[stage[z][chips - s + z]] if z <= s - 1 else entries[0] for z in range(chips)]
    down = [entries[stage[z][s - chips + z]] if z >= chips - s else entries[0] for z in range(chips)]
    wanted = named([list(a) + list(b) for a, b in zip(up, down)])
    return line_sums(wanted, parts, [[received[0]], [received[1]]], [], after)


def scatter_hop(payload, s, chips):
    up, down = line_pairs(range(0, s), 1), line_pairs(range(chips - s, chips), -1)
    if len(payload) == 1:
        both = lax.ppermute(payload[0], "tensor", up + down)
        return [both, both]
    return [lax.ppermute(payload[0], "tensor", up), lax.ppermute(payload[1], "tensor", down)]


def scatter_end(part, received, extra, after):
    entry = part[0].shape[0] - 1
    return line_sums(jnp.array([0, entry], jnp.int32), [part], [list(received)], extra, after, flops=COVER)


def body(
    tokens,
    cotangent,
    gate_weight,
    up_weight,
    down_weight,
    block_task,
    block_fill,
    task_slot,
    inner_correction_weights,
    up_b,
):
    size, groups = lax.axis_size("tensor"), lax.axis_size("dp")
    chips = size // 2
    last, half = chips - 1, chips // 2
    me, group = lax.axis_index("tensor"), lax.axis_index("dp")
    chip, core = me // 2, me % 2
    rows, width = tokens.shape
    count = block_task.shape[0]
    slots, rank = inner_correction_weights.shape[:2]
    distances = [1 << i for i in range(size.bit_length() - 1)]

    def exchange(x, r):
        return lax.ppermute(x, "dp", [(d, d ^ r) for d in range(groups)])

    def from_distance(x, distance):
        return lax.ppermute(x, "tensor", [(i, i ^ distance) for i in range(size)])

    def pairs(table):
        return jnp.stack([2 * table + core, 2 * table + 1 - core], axis=1).reshape(-1).astype(jnp.int32)

    order = pairs(jnp.array(arrival_order(chips), jnp.int32)[chip])
    targets = pairs(jnp.array(send_order(chips), jnp.int32)[chip])

    hop = line_hop(tokens, tokens, 1, chips)
    shards = [tokens, swap_cores(tokens, chips)]
    task_ids = jnp.arange(task_slot.shape[0], dtype=jnp.int32)
    slot = jnp.sum(jnp.where(block_task[:, None] == task_ids[None, :], task_slot[None, :], 0), axis=1)
    wanted, bit = slot, 1
    while bit < groups:
        theirs = exchange(wanted, bit)
        low_side = (group & bit) == 0
        wanted = jnp.concatenate([jnp.where(low_side, wanted, theirs), jnp.where(low_side, theirs, wanted)])
        bit *= 2
    place = wanted - group * slots
    places = jnp.where(jnp.logical_and(place >= 0, place < slots), place, -1)

    left, right, sums, mark = [tokens], [tokens], [], None
    begun = 0
    for j in range(1, chips):
        left.append(hop[0])
        right.append(hop[1])
        if j < last - 1:
            hop = line_hop(left[j], right[j], j + 1, chips)
        mine, mark = stage_shard(chip, left, right, j, chips, [mark] if j > 1 else [])
        if j == 1:
            picked_in, picked_out, mark = pick_slots(places, inner_correction_weights, up_b, [mark])
            factor_in = lax.psum_scatter(picked_in, "dp", scatter_dimension=0, tiled=True)
            factor_out = lax.psum_scatter(picked_out, "dp", scatter_dimension=0, tiled=True)
        if j == last - 1:
            hop = last_hop(mine, chips)
        shards += [mine, swap_cores(mine, chips)]
        if j in (half - 1, last - 1):
            *sums, mark = forward_part(
                order[2 * begun : 2 * j + 2], shards, gate_weight, up_weight, sums, [mark]
            )
            shards, begun = [], j + 1
        if j == last - 1:
            low, mark = low_rank(tokens, factor_in, [mark])
            low, mark = sum_small([low, from_distance(low, 1)], [mark])
            cotangent, mark = copy_both([cotangent], [mark])
    far = [from_distance(low, 2 * k) for k in range(1, chips)]
    cotangent_hop = line_hop(cotangent, cotangent, 1, chips)
    cotangent_other = swap_cores(cotangent, chips)
    gate, up, mark = forward_part(order[2 * begun :], shards, gate_weight, up_weight, sums, [mark])
    low = sum_small([low] + far, [mark])[0]
    live = (jnp.arange(BLOCK, dtype=jnp.int32)[None, :] < block_fill[:, None]).astype(f32)[..., None]
    low_b = (low.reshape(count, BLOCK, rank) * live).astype(bf16).reshape(rows, rank)
    left, right = [cotangent], [cotangent]
    hidden_b, act, slope, mark = activate(gate, up, low_b, factor_out, [mark])
    first = copy_both(cotangent_hop, [mark])
    left.append(first[0])
    right.append(first[1])
    cotangent_hop = line_hop(left[1], right[1], 2, chips)

    def mixed_part(which, after):
        mine, theirs, mark = mixed_parts(targets[which], hidden_b, down_weight, width, after)
        return (mine, swap_cores(theirs, chips)), mark

    mixed = []
    part, mark = mixed_part(slice(0, 2), [first[-1]])
    mixed.append(part)
    part, mark = mixed_part(slice(2, 2 * chips), [mark])
    mixed.append(part)
    shards = [cotangent, cotangent_other]
    for j in range(1, chips):
        if j > 1:
            left.append(cotangent_hop[0])
            right.append(cotangent_hop[1])
            if j < last - 1:
                cotangent_hop = line_hop(left[j], right[j], j + 1, chips)
        value, mark = stage_shard(chip, left, right, j, chips, [mark])
        if j == last - 1:
            cotangent_hop = last_hop(value, chips)
            *payload, mark = scatter_sums(chip, mixed, None, 1, chips, [mark])
            mixed_hop = scatter_hop(payload, 1, chips)
            total, mark = hidden_part(order[: 2 * half], shards[: 2 * half], down_weight, [mark])
        shards += [value, swap_cores(value, chips)]
    *payload, mark = scatter_sums(chip, mixed, mixed_hop, 2, chips, [mark])
    mixed_hop = scatter_hop(payload, 2, chips)
    d_gate, d_up, d_low, out_grad, mark = hidden_gradients(
        order[2 * half :], shards[2 * half :], down_weight, total, act, slope, low_b, factor_out, [mark]
    )

    def item(which, after):
        return item_part(targets[which], d_gate, d_up, gate_weight, up_weight, width, after)

    out_grads = lax.all_gather(out_grad, "dp", axis=0, tiled=True)
    near_low = from_distance(d_low, distances[0])
    theirs, mark = item(slice(1, 2), [mark])
    theirs = swap_cores(theirs, chips)
    d_low, mark = sum_small([d_low, near_low], [mark])
    far_low = from_distance(d_low, distances[1])
    mine, mark = item(slice(0, 1), [mark])
    parts = [(mine, theirs)]
    item_hop = None
    bits = [1 << i for i in range(groups.bit_length() - 1)]
    for j in range(1, chips):
        *payload, mark = scatter_sums(chip, parts, item_hop, j, chips, [mark])
        item_hop = scatter_hop(payload, j, chips)
        if j == 1:
            for s in range(3, chips):
                *payload, mark = scatter_sums(chip, mixed, mixed_hop, s, chips, [mark])
                mixed_hop = scatter_hop(payload, s, chips)
            for distance in distances[2:]:
                d_low, mark = sum_small([d_low, far_low], [mark])
                far_low = from_distance(d_low, distance)
        mine, theirs, mark = item(slice(2 * j, 2 * j + 2), [mark])
        parts.append((mine, swap_cores(theirs, chips)))
        after = [mark] + list(item_hop)
        if j == 1:
            out_sums, mark = slot_sums(places, out_grads, slots, after, flops=COVER)
            in_grad, through, mark = low_rank_gradients(
                block_fill, [d_low, far_low], tokens, factor_in, [mark]
            )
            in_grads = {0: in_grad} | {bit: exchange(in_grad, bit) for bit in bits}
        if j == 2:
            mixed, mark = scatter_end(mixed[-1], mixed_hop, [], after)
            near = copy_small([in_grads[bit] for bit in bits], [mark])
            mark = near[-1]
            in_grads |= dict(zip(bits, near))
            for r in range(1, groups):
                if r not in in_grads:
                    top = 1 << (r.bit_length() - 1)
                    in_grads[r] = exchange(in_grads[top], r ^ top)
    near_places = jnp.concatenate(
        [lax.dynamic_slice_in_dim(places, (group ^ r) * count, count, 0) for r in range(groups)]
    )
    in_grads = jnp.concatenate([in_grads[r] for r in range(groups)])
    in_sums, mark = slot_sums(near_places, in_grads, slots, after, flops=COVER)
    item_derivative = scatter_end(parts[-1], item_hop, [through], [mark])[0]
    return (mixed, item_derivative, in_sums, out_sums)


def solution(mesh):
    return jax.shard_map(
        body,
        mesh=mesh,
        in_specs=(
            P("dp", "tensor"),
            P("dp", "tensor"),
            P(None, "tensor"),
            P(None, "tensor"),
            P("tensor", None),
            P("dp"),
            P("dp"),
            P(),
            P("dp", None, "tensor"),
            P("dp", None, "tensor"),
        ),
        out_specs=(
            P("dp", "tensor"),
            P("dp", "tensor"),
            P("dp", None, "tensor"),
            P("dp", None, "tensor"),
        ),
        check_vma=False,
    )
```

```python
import functools

import jax
import jax.numpy as jnp
from jax import lax
from jax.experimental import pallas as pl
from jax.experimental.pallas import tpu as pltpu
from jax.sharding import PartitionSpec as P

BLOCK = 128
adapter_scale = 0.25
VMEM_LIMIT = 32 * 1024 * 1024
COVER = 1 << 32
f32 = jnp.float32
bf16 = jnp.bfloat16
NT = (((1,), (1,)), ((), ()))


def params():
    return pltpu.CompilerParams(vmem_limit_bytes=VMEM_LIMIT)


def tile_of(size, most=256):
    return next((t for t in range(most, 127, -128) if size % t == 0), size)


def ordered_call(kernel, *, grid, in_specs, out_specs, out_shape, name, flops=1 << 27, prefetch=0, scratch=(), after=(), far=None):
    many = prefetch + len(in_specs)
    outs = len(out_specs)

    def run(*refs):
        mark = refs[many + len(after) + outs]
        mark[...] = jnp.zeros_like(mark)
        kernel(*refs[:many], *refs[many + len(after) : many + len(after) + outs], *refs[many + len(after) + outs + 1 :])

    def shape_of(x):
        return pltpu.HBM(x.shape, x.dtype) if x.shape == far else x

    call = pl.pallas_call(
        run,
        grid_spec=pltpu.PrefetchScalarGridSpec(
            num_scalar_prefetch=prefetch,
            grid=grid,
            in_specs=list(in_specs) + [pl.BlockSpec(memory_space=pl.ANY)] * len(after),
            out_specs=list(out_specs) + [pl.BlockSpec((8, 128), lambda *_: (0, 0))],
            scratch_shapes=list(scratch),
        ),
        out_shape=[shape_of(x) if x.dtype == f32 else x for x in out_shape] + [jax.ShapeDtypeStruct((8, 128), f32)],
        compiler_params=params(),
        cost_estimate=pl.CostEstimate(flops=flops, bytes_accessed=flops // 384, transcendentals=0),
        name=name,
    )
    def place(x):
        hold = x.shape == far and x.dtype == f32 and name != "activate"
        return pltpu.with_memory_space_constraint(x, pltpu.HBM) if hold else x

    return lambda *operands: call(*(place(x) for x in operands), *after)


def adapter_rows(count):
    return [slice(i * BLOCK, (i + 1) * BLOCK) for i in range(count)]


def forward_part(ids, shards, gate_weight, up_weight, sums, after):
    rows, width = shards[0].shape
    hidden = gate_weight.shape[1]
    tile = tile_of(hidden)
    many = len(shards)

    def kernel(ids_ref, *refs):
        xs, gs, us = refs[:many], refs[many : 2 * many], refs[2 * many : 3 * many]
        g = u = None
        if sums:
            g, u = refs[3 * many][...], refs[3 * many + 1][...]
        for x, wg, wu in zip(xs, gs, us):
            a = x[...]
            pg = jnp.dot(a, wg[...], preferred_element_type=f32)
            pu = jnp.dot(a, wu[...], preferred_element_type=f32)
            g, u = (pg, pu) if g is None else (g + pg, u + pu)
        refs[-2][...] = g
        refs[-1][...] = u

    whole = pl.BlockSpec((rows, width), lambda t, ids: (0, 0))
    weights = [pl.BlockSpec((width, tile), lambda t, ids, i=i: (ids[i], t)) for i in range(many)]
    acc = pl.BlockSpec((rows, tile), lambda t, ids: (0, t))
    shape = jax.ShapeDtypeStruct((rows, hidden), f32)
    return ordered_call(
        kernel,
        prefetch=1,
        grid=(hidden // tile,),
        in_specs=[whole] * many + weights + weights + [acc] * len(sums),
        out_specs=[acc, acc],
        out_shape=[shape, shape],
        name="forward_part",
        flops=4 * many * rows * width * hidden,
        after=after,
    )(ids, *shards, *[gate_weight] * many, *[up_weight] * many, *sums)


def activate(gate, up, low_b, factor, after):
    rows, hidden = gate.shape
    tile = tile_of(hidden, 512)
    count, rank = factor.shape[0], factor.shape[1]

    def kernel(g_ref, u_ref, low_ref, b_ref, h_ref, act_ref, slope_ref):
        for i, part in enumerate(adapter_rows(count)):
            g = g_ref[part]
            u = u_ref[part] + adapter_scale * jnp.dot(low_ref[part], b_ref[i], preferred_element_type=f32)
            s = jax.nn.sigmoid(g)
            act = g * s
            act_ref[part] = act
            h_ref[part] = (act * u).astype(bf16)
            slope_ref[part] = u * s * (1.0 + g * (1.0 - s))

    acc = pl.BlockSpec((rows, tile), lambda t: (0, t))
    return ordered_call(
        kernel,
        grid=(hidden // tile,),
        in_specs=[
            acc, acc,
            pl.BlockSpec((rows, rank), lambda t: (0, 0)),
            pl.BlockSpec((count, rank, tile), lambda t: (0, 0, t)),
        ],
        out_specs=[acc, acc, acc],
        out_shape=[
            jax.ShapeDtypeStruct((rows, hidden), bf16),
            jax.ShapeDtypeStruct((rows, hidden), f32),
            jax.ShapeDtypeStruct((rows, hidden), f32),
        ],
        name="activate",
        far=(rows, hidden),
        flops=1 << 31,
        after=after,
    )(gate, up, low_b, factor)


def hidden_product(x_refs, w_refs):
    return functools.reduce(
        jnp.add,
        [lax.dot_general(x[...], w[...], NT, preferred_element_type=f32) for x, w in zip(x_refs, w_refs)],
    )


def hidden_part(ids, shards, down_weight, after):
    rows, width = shards[0].shape
    hidden = down_weight.shape[0]
    tile = tile_of(hidden)
    many = len(shards)

    def kernel(ids_ref, *refs):
        refs[-1][...] = hidden_product(refs[:many], refs[many:-1])

    whole = pl.BlockSpec((rows, width), lambda t, ids: (0, 0))
    weights = [pl.BlockSpec((tile, width), lambda t, ids, i=i: (t, ids[i])) for i in range(many)]
    return ordered_call(
        kernel,
        prefetch=1,
        grid=(hidden // tile,),
        in_specs=[whole] * many + weights,
        out_specs=[pl.BlockSpec((rows, tile), lambda t, ids: (0, t))],
        out_shape=[jax.ShapeDtypeStruct((rows, hidden), f32)],
        name="hidden_part",
        far=(rows, hidden),
        flops=2 * many * rows * width * hidden,
        after=after,
    )(ids, *shards, *([down_weight] * many))


def hidden_gradients(ids, shards, down_weight, total, act, slope, low_b, factor, after):
    rows, width = shards[0].shape
    hidden = down_weight.shape[0]
    tile = tile_of(hidden)
    count, rank = factor.shape[0], factor.shape[1]
    many = len(shards)

    def kernel(ids_ref, *refs):
        d_ref, act_ref, slope_ref, low_ref, b_ref, dg_ref, du_ref, dl_ref, gb_ref = refs[2 * many :]
        d = d_ref[...] + hidden_product(refs[:many], refs[many : 2 * many])
        dg_ref[...] = (d * slope_ref[...]).astype(bf16)
        du = (d * act_ref[...]).astype(bf16)
        du_ref[...] = du

        @pl.when(pl.program_id(0) == 0)
        def _():
            dl_ref[...] = jnp.zeros_like(dl_ref)

        for i, part in enumerate(adapter_rows(count)):
            dl_ref[part] += lax.dot_general(du[part], b_ref[i], NT, preferred_element_type=f32)
            grad = lax.dot_general(low_ref[part], du[part], (((0,), (0,)), ((), ())), preferred_element_type=f32)
            gb_ref[i] = (adapter_scale * grad).astype(bf16)

    whole = pl.BlockSpec((rows, width), lambda t, ids: (0, 0))
    weights = [pl.BlockSpec((tile, width), lambda t, ids, i=i: (t, ids[i])) for i in range(many)]
    acc = pl.BlockSpec((rows, tile), lambda t, ids: (0, t))
    lows = pl.BlockSpec((rows, rank), lambda t, ids: (0, 0))
    factors = pl.BlockSpec((count, rank, tile), lambda t, ids: (0, 0, t))
    return ordered_call(
        kernel,
        prefetch=1,
        grid=(hidden // tile,),
        in_specs=[whole] * many + weights + [acc, acc, acc, lows, factors],
        out_specs=[acc, acc, lows, factors],
        out_shape=[
            jax.ShapeDtypeStruct((rows, hidden), bf16),
            jax.ShapeDtypeStruct((rows, hidden), bf16),
            jax.ShapeDtypeStruct((rows, rank), f32),
            jax.ShapeDtypeStruct((count, rank, hidden), bf16),
        ],
        name="hidden_gradients",
        far=(rows, hidden),
        flops=2 * many * rows * width * hidden,
        after=after,
    )(ids, *shards, *([down_weight] * many), total, act, slope, low_b, factor)


def mixed_parts(ids, x, down_weight, width, after):
    rows, hidden = x.shape
    tile = tile_of(width, 512)
    steps = width // tile
    pairs = ids.shape[0] // 2

    def kernel(ids_ref, x_ref, wa, wb, oa, ob):
        oa[0] = jnp.dot(x_ref[...], wa[...], preferred_element_type=f32).astype(bf16)
        ob[0] = jnp.dot(x_ref[...], wb[...], preferred_element_type=f32).astype(bf16)

    out = pl.BlockSpec((1, rows, tile), lambda j, t, ids: (j, 0, t))
    shape = jax.ShapeDtypeStruct((pairs, rows, width), bf16)
    return ordered_call(
        kernel,
        prefetch=1,
        grid=(pairs, steps),
        in_specs=[
            pl.BlockSpec((rows, hidden), lambda j, t, ids: (0, 0)),
            pl.BlockSpec((hidden, tile), lambda j, t, ids: (0, ids[2 * j] * steps + t)),
            pl.BlockSpec((hidden, tile), lambda j, t, ids: (0, ids[2 * j + 1] * steps + t)),
        ],
        out_specs=[out, out],
        out_shape=[shape, shape],
        name="mixed_parts",
        flops=4 * pairs * rows * width * hidden,
        after=after,
    )(ids, x, down_weight, down_weight)


def item_part(ids, d_gate, d_up, gate_weight, up_weight, width, after):
    rows, hidden = d_gate.shape
    shards = ids.shape[0]
    tile = tile_of(width, 512)
    steps = width // tile

    def kernel(ids_ref, dg, du, *refs):
        for i in range(shards):
            total = lax.dot_general(dg[...], refs[2 * i][...], NT, preferred_element_type=f32)
            total = total + lax.dot_general(du[...], refs[2 * i + 1][...], NT, preferred_element_type=f32)
            refs[2 * shards + i][0] = total.astype(bf16)

    whole = pl.BlockSpec((rows, hidden), lambda t, ids: (0, 0))
    specs = [whole, whole]
    for i in range(shards):
        specs += [pl.BlockSpec((tile, hidden), lambda t, ids, i=i: (ids[i] * steps + t, 0))] * 2
    return ordered_call(
        kernel,
        prefetch=1,
        grid=(steps,),
        in_specs=specs,
        out_specs=[pl.BlockSpec((1, rows, tile), lambda t, ids: (0, 0, t))] * shards,
        out_shape=[jax.ShapeDtypeStruct((1, rows, width), bf16)] * shards,
        name="item_part",
        flops=4 * shards * rows * width * hidden,
        after=after,
    )(ids, d_gate, d_up, *([gate_weight, up_weight] * shards))


def copy_chosen(index, options, after):
    rows, width = options[0].shape
    half = rows // 2

    def kernel(index_ref, *refs):
        for i in range(len(options)):

            @pl.when(index_ref[0] == i)
            def _():
                refs[-1][...] = refs[i][...]

    def block(i):
        return pl.BlockSpec((half, width), lambda t, index: (jnp.where(index[0] == i, t, 0), 0))

    return ordered_call(
        kernel,
        prefetch=1,
        grid=(2,),
        in_specs=[block(i) for i in range(len(options))],
        out_specs=[pl.BlockSpec((half, width), lambda t, index: (t, 0))],
        out_shape=[jax.ShapeDtypeStruct((rows, width), bf16)],
        name="copy_chosen",
        after=after,
    )(index, *options)


def copy_both(arrays, after):
    rows, width = arrays[0].shape
    many = len(arrays)

    def kernel(*refs):
        for i in range(many):
            refs[many + i][...] = refs[i][...]

    block = pl.BlockSpec((rows // 2, width), lambda t: (t, 0))
    return ordered_call(
        kernel,
        grid=(2,),
        in_specs=[block] * many,
        out_specs=[block] * many,
        out_shape=[jax.ShapeDtypeStruct(x.shape, x.dtype) for x in arrays],
        name="copy_both",
        after=after,
    )(*arrays)


def copy_small(arrays, after):
    many = len(arrays)

    def kernel(*refs):
        for i in range(many):
            refs[many + i][...] = refs[i][...]

    block = pl.BlockSpec(arrays[0].shape, lambda t: (0,) * arrays[0].ndim)
    return ordered_call(
        kernel,
        grid=(1,),
        in_specs=[block] * many,
        out_specs=[block] * many,
        out_shape=[jax.ShapeDtypeStruct(x.shape, x.dtype) for x in arrays],
        name="copy_small",
        after=after,
    )(*arrays)


def line_sums(wanted, parts, received, extra, after, flops=1 << 27):
    rows, width = parts[0][0].shape[1:]
    half = rows // 2
    outs = len(received)
    arrays = [x for pair in parts for x in pair]
    others = [x for group in received for x in group] + extra

    def kernel(wanted_ref, *refs):
        step = 0
        ins = refs[: outs * len(arrays)]
        adds = list(refs[outs * len(arrays) : -outs])
        for k in range(outs):
            terms = [adds.pop(0)[...].astype(f32) for _ in received[k]]
            terms += [x[...] for x in adds[len(adds) - len(extra) :]] if k == outs - 1 else []

            for i in range(len(parts)):

                @pl.when(wanted_ref[2 * k] == i)
                def _():
                    mine, theirs = ins[step + 2 * i], ins[step + 2 * i + 1]
                    total = functools.reduce(jnp.add, terms, mine[0].astype(f32) + theirs[0].astype(f32))
                    refs[len(refs) - outs + k][...] = total.astype(bf16)

            step += len(arrays)

    def block(k, i):
        def where(t, wanted):
            hit = wanted[2 * k] == i // 2
            return (jnp.where(hit, wanted[2 * k + 1], 0), jnp.where(hit, t, 0), 0)

        return pl.BlockSpec((1, half, width), where)

    flat = pl.BlockSpec((half, width), lambda t, wanted: (t, 0))
    return ordered_call(
        kernel,
        prefetch=1,
        grid=(2,),
        in_specs=[block(k, i) for k in range(outs) for i in range(len(arrays))] + [flat] * len(others),
        out_specs=[flat] * outs,
        out_shape=[jax.ShapeDtypeStruct((rows, width), bf16)] * outs,
        name="line_sums",
        flops=flops,
        after=after,
    )(wanted, *arrays * outs, *others)


def sum_small(arrays, after):
    def kernel(*refs):
        refs[-1][...] = functools.reduce(jnp.add, [x[...] for x in refs[:-1]])

    block = pl.BlockSpec(arrays[0].shape, lambda t: (0, 0))
    return ordered_call(
        kernel,
        grid=(1,),
        in_specs=[block] * len(arrays),
        out_specs=[block],
        out_shape=[jax.ShapeDtypeStruct(arrays[0].shape, f32)],
        name="sum_small",
        after=after,
    )(*arrays)


def low_rank(tokens, factor, after):
    rows, width = tokens.shape
    count, rank = factor.shape[:2]

    def kernel(x_ref, a_ref, o_ref):
        for i, part in enumerate(adapter_rows(count)):
            o_ref[part] = lax.dot_general(x_ref[part], a_ref[i], NT, preferred_element_type=f32)

    return ordered_call(
        kernel,
        grid=(1,),
        in_specs=[
            pl.BlockSpec((rows, width), lambda t: (0, 0)),
            pl.BlockSpec(factor.shape, lambda t: (0, 0, 0)),
        ],
        out_specs=[pl.BlockSpec((rows, rank), lambda t: (0, 0))],
        out_shape=[jax.ShapeDtypeStruct((rows, rank), f32)],
        name="low_rank",
        after=after,
    )(tokens, factor)


def low_rank_gradients(fill, lows, tokens, factor, after):
    rows, width = tokens.shape
    count, rank = factor.shape[:2]

    def kernel(fill_ref, x_ref, a_ref, *refs):
        d_low = functools.reduce(jnp.add, [x[...] for x in refs[:-2]])
        for i, part in enumerate(adapter_rows(count)):
            alive = lax.broadcasted_iota(jnp.int32, (BLOCK, rank), 0) < fill_ref[i]
            d = jnp.where(alive, adapter_scale * d_low[part], 0.0).astype(bf16)
            grad = lax.dot_general(d, x_ref[part], (((0,), (0,)), ((), ())), preferred_element_type=f32)
            refs[-2][i] = grad.astype(bf16)
            refs[-1][part] = jnp.dot(d, a_ref[i], preferred_element_type=f32)

    block = pl.BlockSpec(factor.shape, lambda t, fill: (0, 0, 0))
    whole = pl.BlockSpec((rows, width), lambda t, fill: (0, 0))
    return ordered_call(
        kernel,
        prefetch=1,
        grid=(1,),
        in_specs=[whole, block] + [pl.BlockSpec((rows, rank), lambda t, fill: (0, 0))] * len(lows),
        out_specs=[block, whole],
        out_shape=[jax.ShapeDtypeStruct(factor.shape, bf16), jax.ShapeDtypeStruct((rows, width), f32)],
        name="low_rank_gradients",
        after=after,
    )(fill, tokens, factor, *lows)


def pick_slots(places, in_factor, out_factor, after):
    many = places.shape[0]

    def kernel(places_ref, a_ref, b_ref, oa, ob):
        held = places_ref[pl.program_id(0)] >= 0

        @pl.when(held)
        def _():
            oa[...] = a_ref[...]
            ob[...] = b_ref[...]

        @pl.when(~held)
        def _():
            oa[...] = jnp.zeros_like(oa)
            ob[...] = jnp.zeros_like(ob)

    def block(factor):
        return (1,) + factor.shape[1:]

    picked = [pl.BlockSpec(block(f), lambda i, ids: (jnp.maximum(ids[i], 0), 0, 0)) for f in (in_factor, out_factor)]
    out = [pl.BlockSpec(block(f), lambda i, ids: (i, 0, 0)) for f in (in_factor, out_factor)]
    return ordered_call(
        kernel,
        prefetch=1,
        grid=(many,),
        in_specs=picked,
        out_specs=out,
        out_shape=[jax.ShapeDtypeStruct((many,) + f.shape[1:], bf16) for f in (in_factor, out_factor)],
        name="pick_slots",
        after=after,
    )(places, in_factor, out_factor)


def slot_sums(places, grads, slots, after, flops=1 << 27):
    total_blocks, rank, width = grads.shape

    def kernel(places_ref, *rest):
        ins, out, total = rest
        out[...] = jnp.zeros_like(out)
        for i in range(total_blocks):
            place = places_ref[i]
            earlier = functools.reduce(jnp.logical_or, [places_ref[j] == place for j in range(i)], False)
            later = functools.reduce(jnp.logical_or, [places_ref[j] == place for j in range(i + 1, total_blocks)], False)
            here = ins.at[i]
            held = place >= 0

            @pl.when(held & ~jnp.logical_or(earlier, later))
            def _():
                out[pl.ds(jnp.maximum(place, 0), 1)] = here[...][None]

            @pl.when(held & ~jnp.asarray(earlier) & later)
            def _():
                total[...] = here[...].astype(f32)
                for j in range(i + 1, total_blocks):

                    @pl.when(places_ref[j] == place)
                    def _():
                        total[...] += ins[j].astype(f32)

                out[pl.ds(jnp.maximum(place, 0), 1)] = total[...].astype(bf16)[None]

    return ordered_call(
        kernel,
        prefetch=1,
        grid=(1,),
        in_specs=[pl.BlockSpec((total_blocks, rank, width), lambda s, ids: (0, 0, 0))],
        out_specs=[pl.BlockSpec((slots, rank, width), lambda s, ids: (0, 0, 0))],
        scratch=[pltpu.VMEM((rank, width), f32)],
        out_shape=[jax.ShapeDtypeStruct((slots, rank, width), bf16)],
        name="slot_sums",
        flops=flops,
        after=after,
    )(places, grads)


def line_pairs(sources, step):
    return [(2 * z + core, 2 * (z + step) + core) for z in sources for core in (0, 1)]


def swap_cores(x, chips):
    return lax.ppermute(x, "tensor", [(i, i ^ 1) for i in range(2 * chips)])


def arrival_order(chips):
    order = []
    for z in range(chips):
        up, down = list(range(z + 1, chips)), list(range(z - 1, -1, -1))
        order.append([z] + (up + down if 2 * z < chips else down + up))
    return order


def line_hop(left, right, s, chips):
    return [
        lax.ppermute(left, "tensor", line_pairs(range(s - 1, chips - 1), 1)),
        lax.ppermute(right, "tensor", line_pairs(range(1, chips - s + 1), -1)),
    ]


def last_hop(shard, chips):
    both = lax.ppermute(shard, "tensor", line_pairs([chips - 2], 1) + line_pairs([1], -1))
    return [both, both]


def stage_shard(chip, left, right, j, chips, after):
    options, where = [], []
    for z, row in enumerate(arrival_order(chips)):
        value = left[z - row[j]] if row[j] <= z else right[row[j] - z]
        spot = next((i for i, option in enumerate(options) if option is value), len(options))
        if spot == len(options):
            options.append(value)
        where.append(spot)
    return copy_chosen(jnp.array(where, jnp.int32)[chip][None], options, after)


def send_order(chips):
    order = []
    for z in range(chips):
        due = []
        for s in range(1, chips):
            if z <= s - 1:
                due.append(chips - s + z)
            if z >= chips - s:
                due.append(s - chips + z)
        order.append(due + [z])
    return order


def scatter_sums(chip, parts, received, s, chips, after):
    stage = [{d: j for j, d in enumerate(row)} for row in send_order(chips)]
    entries = [(i, k) for i, pair in enumerate(parts) for k in range(pair[0].shape[0])]

    def named(table):
        return jnp.array(table, jnp.int32)[chip]

    if s == 1:
        wanted = named([entries[0]] * chips)
        return line_sums(wanted, parts[:1], [[]], [], after)
    up = [entries[stage[z][chips - s + z]] if z <= s - 1 else entries[0] for z in range(chips)]
    down = [entries[stage[z][s - chips + z]] if z >= chips - s else entries[0] for z in range(chips)]
    wanted = named([list(a) + list(b) for a, b in zip(up, down)])
    return line_sums(wanted, parts, [[received[0]], [received[1]]], [], after)


def scatter_hop(payload, s, chips):
    up, down = line_pairs(range(0, s), 1), line_pairs(range(chips - s, chips), -1)
    if len(payload) == 1:
        both = lax.ppermute(payload[0], "tensor", up + down)
        return [both, both]
    return [lax.ppermute(payload[0], "tensor", up), lax.ppermute(payload[1], "tensor", down)]


def scatter_end(part, received, extra, after):
    entry = part[0].shape[0] - 1
    return line_sums(jnp.array([0, entry], jnp.int32), [part], [list(received)], extra, after, flops=COVER)


def body(
    tokens,
    cotangent,
    gate_weight,
    up_weight,
    down_weight,
    block_task,
    block_fill,
    task_slot,
    inner_correction_weights,
    up_b,
):
    size, groups = lax.axis_size("tensor"), lax.axis_size("dp")
    chips = size // 2
    last, half = chips - 1, chips // 2
    me, group = lax.axis_index("tensor"), lax.axis_index("dp")
    chip, core = me // 2, me % 2
    rows, width = tokens.shape
    count = block_task.shape[0]
    slots, rank = inner_correction_weights.shape[:2]
    distances = [1 << i for i in range(size.bit_length() - 1)]

    def exchange(x, r):
        return lax.ppermute(x, "dp", [(d, d ^ r) for d in range(groups)])

    def from_distance(x, distance):
        return lax.ppermute(x, "tensor", [(i, i ^ distance) for i in range(size)])

    def pairs(table):
        return jnp.stack([2 * table + core, 2 * table + 1 - core], axis=1).reshape(-1).astype(jnp.int32)

    order = pairs(jnp.array(arrival_order(chips), jnp.int32)[chip])
    targets = pairs(jnp.array(send_order(chips), jnp.int32)[chip])

    hop = line_hop(tokens, tokens, 1, chips)
    shards = [tokens, swap_cores(tokens, chips)]
    task_ids = jnp.arange(task_slot.shape[0], dtype=jnp.int32)
    slot = jnp.sum(jnp.where(block_task[:, None] == task_ids[None, :], task_slot[None, :], 0), axis=1)
    wanted, bit = slot, 1
    while bit < groups:
        theirs = exchange(wanted, bit)
        low_side = (group & bit) == 0
        wanted = jnp.concatenate([jnp.where(low_side, wanted, theirs), jnp.where(low_side, theirs, wanted)])
        bit *= 2
    place = wanted - group * slots
    places = jnp.where(jnp.logical_and(place >= 0, place < slots), place, -1)

    left, right, sums, mark = [tokens], [tokens], [], None
    begun = 0
    for j in range(1, chips):
        left.append(hop[0])
        right.append(hop[1])
        if j < last - 1:
            hop = line_hop(left[j], right[j], j + 1, chips)
        mine, mark = stage_shard(chip, left, right, j, chips, [mark] if j > 1 else [])
        if j == 1:
            picked_in, picked_out, mark = pick_slots(places, inner_correction_weights, up_b, [mark])
            factor_in = lax.psum_scatter(picked_in, "dp", scatter_dimension=0, tiled=True)
            factor_out = lax.psum_scatter(picked_out, "dp", scatter_dimension=0, tiled=True)
        if j == last - 1:
            hop = last_hop(mine, chips)
        shards += [mine, swap_cores(mine, chips)]
        if j == half - 1:
            *sums, mark = forward_part(
                order[2 * begun : 2 * j + 2], shards, gate_weight, up_weight, sums, [mark]
            )
            shards, begun = [], j + 1
        if j == last - 1:
            low, mark = low_rank(tokens, factor_in, [mark])
            low, mark = sum_small([low, from_distance(low, 1)], [mark])
            cotangent, mark = copy_both([cotangent], [mark])
    far = [from_distance(low, 2 * k) for k in range(1, chips)]
    cotangent_hop = line_hop(cotangent, cotangent, 1, chips)
    cotangent_other = swap_cores(cotangent, chips)
    gate, up, mark = forward_part(order[2 * begun :], shards, gate_weight, up_weight, sums, [mark])
    low = sum_small([low] + far, [mark])[0]
    live = (jnp.arange(BLOCK, dtype=jnp.int32)[None, :] < block_fill[:, None]).astype(f32)[..., None]
    low_b = (low.reshape(count, BLOCK, rank) * live).astype(bf16).reshape(rows, rank)
    left, right = [cotangent], [cotangent]
    hidden_b, act, slope, mark = activate(gate, up, low_b, factor_out, [mark])
    first = copy_both(cotangent_hop, [mark])
    left.append(first[0])
    right.append(first[1])
    cotangent_hop = line_hop(left[1], right[1], 2, chips)

    def mixed_part(which, after):
        mine, theirs, mark = mixed_parts(targets[which], hidden_b, down_weight, width, after)
        return (mine, swap_cores(theirs, chips)), mark

    mixed = []
    part, mark = mixed_part(slice(0, 2), [first[-1]])
    mixed.append(part)
    part, mark = mixed_part(slice(2, 2 * chips), [mark])
    mixed.append(part)
    shards = [cotangent, cotangent_other]
    for j in range(1, chips):
        if j > 1:
            left.append(cotangent_hop[0])
            right.append(cotangent_hop[1])
            if j < last - 1:
                cotangent_hop = line_hop(left[j], right[j], j + 1, chips)
        value, mark = stage_shard(chip, left, right, j, chips, [mark])
        if j == last - 1:
            cotangent_hop = last_hop(value, chips)
            *payload, mark = scatter_sums(chip, mixed, None, 1, chips, [mark])
            mixed_hop = scatter_hop(payload, 1, chips)
            total, mark = hidden_part(order[: 2 * half], shards[: 2 * half], down_weight, [mark])
        shards += [value, swap_cores(value, chips)]
    *payload, mark = scatter_sums(chip, mixed, mixed_hop, 2, chips, [mark])
    mixed_hop = scatter_hop(payload, 2, chips)
    d_gate, d_up, d_low, out_grad, mark = hidden_gradients(
        order[2 * half :], shards[2 * half :], down_weight, total, act, slope, low_b, factor_out, [mark]
    )

    def item(which, after):
        return item_part(targets[which], d_gate, d_up, gate_weight, up_weight, width, after)

    out_grads = lax.all_gather(out_grad, "dp", axis=0, tiled=True)
    near_low = from_distance(d_low, distances[0])
    theirs, mark = item(slice(1, 2), [mark])
    theirs = swap_cores(theirs, chips)
    d_low, mark = sum_small([d_low, near_low], [mark])
    far_low = from_distance(d_low, distances[1])
    mine, mark = item(slice(0, 1), [mark])
    parts = [(mine, theirs)]
    item_hop = None
    bits = [1 << i for i in range(groups.bit_length() - 1)]
    for j in range(1, chips):
        *payload, mark = scatter_sums(chip, parts, item_hop, j, chips, [mark])
        item_hop = scatter_hop(payload, j, chips)
        if j == 1:
            for s in range(3, chips):
                *payload, mark = scatter_sums(chip, mixed, mixed_hop, s, chips, [mark])
                mixed_hop = scatter_hop(payload, s, chips)
            for distance in distances[2:]:
                d_low, mark = sum_small([d_low, far_low], [mark])
                far_low = from_distance(d_low, distance)
        mine, theirs, mark = item(slice(2 * j, 2 * j + 2), [mark])
        parts.append((mine, swap_cores(theirs, chips)))
        after = [mark] + list(item_hop)
        if j == 1:
            out_sums, mark = slot_sums(places, out_grads, slots, after, flops=COVER)
            in_grad, through, mark = low_rank_gradients(
                block_fill, [d_low, far_low], tokens, factor_in, [mark]
            )
            in_grads = {0: in_grad} | {bit: exchange(in_grad, bit) for bit in bits}
        if j == 2:
            mixed, mark = scatter_end(mixed[-1], mixed_hop, [], after)
            near = copy_small([in_grads[bit] for bit in bits], [mark])
            mark = near[-1]
            in_grads |= dict(zip(bits, near))
            for r in range(1, groups):
                if r not in in_grads:
                    top = 1 << (r.bit_length() - 1)
                    in_grads[r] = exchange(in_grads[top], r ^ top)
    near_places = jnp.concatenate(
        [lax.dynamic_slice_in_dim(places, (group ^ r) * count, count, 0) for r in range(groups)]
    )
    in_grads = jnp.concatenate([in_grads[r] for r in range(groups)])
    in_sums, mark = slot_sums(near_places, in_grads, slots, after, flops=COVER)
    item_derivative = scatter_end(parts[-1], item_hop, [through], [mark])[0]
    return (mixed, item_derivative, in_sums, out_sums)


def solution(mesh):
    return jax.shard_map(
        body,
        mesh=mesh,
        in_specs=(
            P("dp", "tensor"),
            P("dp", "tensor"),
            P(None, "tensor"),
            P(None, "tensor"),
            P("tensor", None),
            P("dp"),
            P("dp"),
            P(),
            P("dp", None, "tensor"),
            P("dp", None, "tensor"),
        ),
        out_specs=(
            P("dp", "tensor"),
            P("dp", "tensor"),
            P("dp", None, "tensor"),
            P("dp", None, "tensor"),
        ),
        check_vma=False,
    )
```
